256 devices in a mesh: wide: 64 (over z, x, core), narrow: 4 (over y).
Axes of the slice: x: 4, y: 4, z: 8, core: 2. Of those that a mesh axis runs over, the one named last changes fastest.
Arguments:
- gebhart: float32 [16384, 16384], P('wide', 'narrow'), may hold values from 0 to 2
- change: float32 [16384, 128], P('narrow'), may hold values from -0.0007324219 to 0.0007324219
- moved_nodes: int32 [128], replicated, may hold values from 0 to 16383, as said below
Outputs:
- updated: float32 [16384, 16384], P('wide', 'narrow')
The draws below stay inside these ranges and needn't reach their ends.
Inputs may be any that keep to these rules, and one draw needn't show every extreme that they name: `moved_nodes`: distinct node indices.
All inputs are finite; a program needn't handle non-finite values.
Results may differ from the reference program's by a relative error of at most 0.00005.
Values sent between devices are 32-bit elements; how exact they have to be, the bound alone decides.
No kernel may reach another device: no remote copies, remote signals or barrier semaphores. Data moves between devices by JAX's collectives and lax.ppermute only.
A program may use at most 64 MiB of HBM per device.

```python
import jax
import jax.numpy as jnp
from jax import lax

NODES = 16384
MOVED = 128


def draw_moved_nodes(key, part):
    key = jax.random.fold_in(key, 7)
    first, second = jax.random.split(key)
    inner = jax.random.permutation(first, NODES - 2)[:MOVED - 2] + 1
    ends = jnp.array([0, NODES - 1], dtype=jnp.int32)
    chosen = jnp.concatenate([inner.astype(jnp.int32), ends])
    return jax.random.permutation(second, chosen).astype(jnp.int32)


def block_scale(key, dims, shards, low, largest):
    factor_of = 1.0
    for position, parts in shards:
        draws = jax.random.uniform(jax.random.fold_in(jax.random.fold_in(key, 6), position), (parts,), jnp.float32, low / len(shards), largest / len(shards))
        factor_of = factor_of * jnp.repeat(jnp.exp(draws), dims[position] // parts).reshape((-1,) + (1,) * (len(dims) - 1 - position))
    return factor_of


def centred(key, shape, deviation, reach, shards=(), kind=jnp.bfloat16):
    entries = jax.random.normal(key, shape, jnp.float32) * deviation
    if len(shards) > 0:
        entries = block_scale(key, shape, shards, -0.22, 0.18) * entries
    return jnp.clip(entries, min=-reach, max=reach).astype(kind)


def setup_inputs(seed: int = 0) -> dict:
    arg_keys = jax.random.split(jax.random.key(seed), 4)
    gebhart = jnp.clip(2.0 * jax.random.uniform(arg_keys[0], (NODES, NODES), jnp.float32) ** block_scale(arg_keys[0], (NODES, NODES), ((0, 64), (1, 4)), -0.2, 0.2), 0.0, 2.0)
    change = centred(arg_keys[1], (NODES, MOVED), (4096 * NODES) ** -0.5, 0.0007324219, ((0, 4),), jnp.float32)
    moved_nodes = draw_moved_nodes(jax.random.fold_in(arg_keys[3], 71), 0)
    return dict(gebhart=gebhart, change=change, moved_nodes=moved_nodes)


def reference(gebhart, change, moved_nodes):
    high = lax.Precision.HIGHEST
    response = jnp.dot(gebhart.astype(jnp.float32), change.astype(jnp.float32), preferred_element_type=jnp.float32, precision=high)
    rows_moved = jnp.take(gebhart, moved_nodes.astype(jnp.int32), axis=0)
    capacitance = jnp.eye(MOVED, dtype=jnp.float32) - jnp.take(response, moved_nodes.astype(jnp.int32), axis=0)
    normal = jnp.dot(capacitance, capacitance.T, precision=high)
    factor = jnp.linalg.cholesky(normal)
    right = jnp.dot(capacitance, response.T, precision=high)
    solved = jax.scipy.linalg.cho_solve((factor, True), right).T
    return gebhart + jnp.dot(solved.astype(jnp.float32), rows_moved.astype(jnp.float32), preferred_element_type=jnp.float32, precision=high)
```

```python
import functools

import jax
import jax.numpy as jnp
from jax import lax
from jax.experimental import pallas as pl
from jax.experimental.pallas import tpu as pltpu
from jax.sharding import PartitionSpec as P

CORES = 2
XS = 4


def pick_kernel(moved_ref, place_ref, g_ref, keep_ref, send_ref, sem):
    rows_local = g_ref.shape[0]
    quarters, half, width = keep_ref.shape
    first = place_ref[0]
    core = place_ref[1]

    def copies(k, act):
        local = moved_ref[k] - first
        owned = jnp.logical_and(local >= 0, local < rows_local)
        side = k // half
        row = k - side * half
        for target, here in ((keep_ref, side == core), (send_ref, side != core)):
            @pl.when(jnp.logical_and(owned, here))
            def _():
                for q in range(quarters):
                    act(pltpu.make_async_copy(
                        g_ref.at[pl.ds(local, 1), pl.ds(q * width, width)],
                        target.at[q, pl.ds(row, 1), :],
                        sem,
                    ))

    def start(k, carry):
        copies(k, lambda copy: copy.start())
        return carry

    def wait(k, carry):
        copies(k, lambda copy: copy.wait())
        return carry

    lax.fori_loop(0, 2 * half, start, 0)
    lax.fori_loop(0, 2 * half, wait, 0)


def pick(gebhart, moved_nodes, place, half, width):
    shape = jax.ShapeDtypeStruct((XS, half, width), jnp.float32)
    return pl.pallas_call(
        pick_kernel,
        out_shape=(shape, shape),
        in_specs=[
            pl.BlockSpec(memory_space=pltpu.SMEM),
            pl.BlockSpec(memory_space=pltpu.SMEM),
            pl.BlockSpec(memory_space=pl.ANY),
        ],
        out_specs=(pl.BlockSpec(memory_space=pl.ANY), pl.BlockSpec(memory_space=pl.ANY)),
        scratch_shapes=[pltpu.SemaphoreType.DMA],
        name="pick_rows",
    )(moved_nodes, place, gebhart)


def split(value):
    high = value.astype(jnp.bfloat16)
    low = (value - high.astype(jnp.float32)).astype(jnp.bfloat16)
    return high, low


def update_kernel(column_ref, core_ref, solved_ref, g_ref, *refs):
    mine, theirs, out_ref = refs[:XS], refs[XS:2 * XS], refs[2 * XS]
    half = mine[0].shape[0]
    step = pl.program_id(0)
    core = core_ref[0]
    s_low_half = solved_ref[:, :half]
    s_high_half = solved_ref[:, half:]
    s_mine = jnp.where(core == 0, s_low_half, s_high_half)
    s_theirs = jnp.where(core == 0, s_high_half, s_low_half)
    s_high, s_low = split(jnp.concatenate([s_mine, s_theirs], axis=1))
    left = jnp.concatenate([s_high, s_low, s_high], axis=1)
    for j in range(XS):
        @pl.when(step == j)
        def _():
            r_high, r_low = split(jnp.concatenate([mine[j][...], theirs[j][...]], axis=0))
            right = jnp.concatenate([r_high, r_high, r_low], axis=0)
            out_ref[...] = g_ref[...] + jnp.dot(left, right, preferred_element_type=jnp.float32)


def update(gebhart, solved, mine, theirs, columns, core):
    rows, nodes = gebhart.shape
    half, width = mine[0].shape
    count = solved.shape[1]
    piece = pl.BlockSpec((half, width), lambda i, col, core: (0, 0))
    block = pl.BlockSpec((rows, width), lambda i, col, core: (0, col[i]))
    return pl.pallas_call(
        update_kernel,
        out_shape=jax.ShapeDtypeStruct((rows, nodes), jnp.float32),
        grid_spec=pltpu.PrefetchScalarGridSpec(
            num_scalar_prefetch=2,
            grid=(XS,),
            in_specs=[pl.BlockSpec((rows, count), lambda i, col, core: (0, 0)), block] + [piece] * (2 * XS),
            out_specs=block,
        ),
        compiler_params=pltpu.CompilerParams(vmem_limit_bytes=40 * 1024 * 1024),
        name="update_rows",
    )(columns, core, solved, gebhart, *mine, *theirs)


def invert(touched):
    high = lax.Precision.HIGHEST
    count = touched.shape[0]
    capacitance = jnp.eye(count, dtype=jnp.float32) - touched
    normal = jnp.dot(capacitance, capacitance.T, precision=high)
    factor = jnp.linalg.cholesky(normal)
    return jax.scipy.linalg.cho_solve((factor, True), capacitance)


def body(wide, narrow, gebhart, change, moved_nodes):
    high = lax.Precision.HIGHEST
    rows_local, width_local = gebhart.shape
    count = moved_nodes.shape[0]
    half = count // CORES
    zs = wide // (CORES * XS)
    width = width_local // XS
    group = half // zs
    me = lax.axis_index("wide")
    core = me % CORES
    x = (me // CORES) % XS
    z = me // (CORES * XS)

    def along(step):
        return [(i, step(i // (CORES * XS), (i // CORES) % XS, i % CORES)) for i in range(wide)]

    def index(z, x, c):
        return (z * XS + x) * CORES + c

    swap = along(lambda z, x, c: index(z, x, (c + 1) % CORES))
    shift_x = [along(lambda z, x, c, d=d: index(z, (x + d) % XS, c)) for d in range(XS)]
    z_groups = [[index(z, x, c) for z in range(zs)] for x in range(XS) for c in range(CORES)]

    owner = moved_nodes // rows_local
    owner_half = lax.dynamic_slice(owner, (core * half,), (half,))
    owner_core = owner_half % CORES
    owner_x = (owner_half // CORES) % XS
    owner_z = owner_half // (CORES * XS)

    place = jnp.stack([me * rows_local, core]).astype(jnp.int32)
    keep, send = pick(gebhart, moved_nodes, place, half, width)
    got = lax.ppermute(send, "wide", swap)

    partial_value = jnp.dot(gebhart, change, preferred_element_type=jnp.float32, precision=lax.Precision.HIGH)
    response = partial_value
    for d in range(1, narrow):
        response = response + lax.ppermute(partial_value, "narrow", [(i, (i + d) % narrow) for i in range(narrow)])
    positions = me * rows_local + lax.broadcasted_iota(jnp.int32, (count, rows_local), 1)
    select = (moved_nodes[:, None] == positions).astype(jnp.float32)
    terms = jnp.dot(select, response, preferred_element_type=jnp.float32, precision=high)
    terms_mine = lax.dynamic_slice(terms, (core * half, 0), (half, count))
    terms_theirs = lax.dynamic_slice(terms, ((1 - core) * half, 0), (half, count))
    terms_chip = terms_mine + lax.ppermute(terms_theirs, "wide", swap)
    terms_x = terms_chip
    for d in range(1, XS):
        terms_x = terms_x + lax.ppermute(terms_chip, "wide", shift_x[d])

    from_mine = (owner_core == core)[:, None]
    slots = []
    for d in range(XS):
        q = (x + d) % XS
        kept = lax.dynamic_index_in_dim(keep, q, 0, keepdims=False)
        other = lax.dynamic_index_in_dim(got, q, 0, keepdims=False)
        slots.append(jnp.where(from_mine, kept, other))
    rows_x = slots[0]
    far = ((x - owner_x) % XS)[:, None]
    for d in range(1, XS):
        rows_x = jnp.where(far == d, lax.ppermute(slots[d], "wide", shift_x[d]), rows_x)

    both = jnp.concatenate([rows_x, terms_x], axis=1).reshape(zs, group, width + count)
    both = lax.all_to_all(both, "wide", 0, 0, axis_index_groups=z_groups)
    owner_z_mine = lax.dynamic_slice(owner_z, (z * group,), (group,))
    chosen = owner_z_mine[None, :, None] == lax.broadcasted_iota(jnp.int32, (zs, 1, 1), 0)
    mine = jnp.sum(jnp.where(chosen, both, 0.0), axis=0)
    both = lax.all_to_all(jnp.broadcast_to(mine[None], (zs,) + mine.shape), "wide", 0, 0, axis_index_groups=z_groups)
    both = both.reshape(half, width + count)

    touched_mine = both[:, width:]
    touched_theirs = lax.ppermute(touched_mine, "wide", swap)
    touched = jnp.where(core == 0, jnp.concatenate([touched_mine, touched_theirs]), jnp.concatenate([touched_theirs, touched_mine]))

    piece = both[:, :width]
    pieces = [piece] + [lax.ppermute(piece, "wide", shift_x[d]) for d in range(1, XS)]
    theirs = [lax.ppermute(p, "wide", swap) for p in pieces]
    columns = jnp.stack([(x - d) % XS for d in range(XS)]).astype(jnp.int32)

    inverse = invert(touched)
    solved = jnp.dot(response, inverse.T, precision=high)
    return update(gebhart, solved, pieces, theirs, columns, core.reshape(1).astype(jnp.int32))


def solution(mesh):
    return jax.shard_map(
        functools.partial(body, mesh.shape["wide"], mesh.shape["narrow"]),
        mesh=mesh,
        in_specs=(P("wide", "narrow"), P("narrow", None), P()),
        out_specs=P("wide", "narrow"),
        check_vma=False,
    )
```

```python
import functools

import jax
import jax.numpy as jnp
from jax import lax
from jax.experimental import pallas as pl
from jax.experimental.pallas import tpu as pltpu
from jax.sharding import PartitionSpec as P

HIGHEST = lax.Precision.HIGHEST
CORES = 2
XS = 4


def pick_kernel(moved_ref, g_ref, keep_ref, send_ref, sem):
    rows_local = g_ref.shape[0]
    quarters, half, width = keep_ref.shape
    me = lax.axis_index("wide")
    first = me * rows_local
    core = me % CORES

    def copy(local, target, row, q):
        return pltpu.make_async_copy(
            g_ref.at[pl.ds(local, 1), pl.ds(q * width, width)], target.at[q, pl.ds(row, 1), :], sem
        )

    total = 0
    for side in range(CORES):
        def start(row, found, side=side):
            local = moved_ref[side * half + row] - first
            owned = jnp.logical_and(local >= 0, local < rows_local)

            @pl.when(owned)
            def _():
                @pl.when(core == side)
                def _():
                    for q in range(quarters):
                        copy(local, keep_ref, row, q).start()

                @pl.when(core != side)
                def _():
                    for q in range(quarters):
                        copy(local, send_ref, row, q).start()

            return found + jnp.where(owned, 1, 0)

        total = lax.fori_loop(0, half, start, total, unroll=8)

    def wait(i, carry):
        for q in range(quarters):
            copy(0, keep_ref, 0, q).wait()
        return carry

    lax.fori_loop(0, total, wait, 0)


def pick(gebhart, moved_nodes, half, width):
    shape = jax.ShapeDtypeStruct((XS, half, width), jnp.float32)
    return pl.pallas_call(
        pick_kernel,
        out_shape=(shape, shape),
        in_specs=[pl.BlockSpec(memory_space=pltpu.SMEM), pl.BlockSpec(memory_space=pl.ANY)],
        out_specs=(pl.BlockSpec(memory_space=pl.ANY), pl.BlockSpec(memory_space=pl.ANY)),
        scratch_shapes=[pltpu.SemaphoreType.DMA],
        compiler_params=pltpu.CompilerParams(vmem_limit_bytes=60 * 1024 * 1024),
        name="pick_rows",
    )(moved_nodes, gebhart)


def split(value):
    high = value.astype(jnp.bfloat16)
    low = (value - high.astype(jnp.float32)).astype(jnp.bfloat16)
    return high, low


def pair_inverse(p, q, s):
    scale = 1.0 / (p * s - q * q)
    return s * scale, -q * scale, p * scale


def quad_inverse(e):
    a, b, c = pair_inverse(e[0][0], e[0][1], e[1][1])
    t = [[a * e[0][2] + b * e[1][2], a * e[0][3] + b * e[1][3]], [b * e[0][2] + c * e[1][2], b * e[0][3] + c * e[1][3]]]
    s22 = e[2][2] - (e[0][2] * t[0][0] + e[1][2] * t[1][0])
    s23 = e[2][3] - (e[0][2] * t[0][1] + e[1][2] * t[1][1])
    s33 = e[3][3] - (e[0][3] * t[0][1] + e[1][3] * t[1][1])
    f, g, h = pair_inverse(s22, s23, s33)
    w = [[t[0][0] * f + t[0][1] * g, t[0][0] * g + t[0][1] * h], [t[1][0] * f + t[1][1] * g, t[1][0] * g + t[1][1] * h]]
    i00 = a + w[0][0] * t[0][0] + w[0][1] * t[0][1]
    i01 = b + w[0][0] * t[1][0] + w[0][1] * t[1][1]
    i11 = c + w[1][0] * t[1][0] + w[1][1] * t[1][1]
    return [
        [i00, i01, -w[0][0], -w[0][1]],
        [i01, i11, -w[1][0], -w[1][1]],
        [-w[0][0], -w[1][0], f, g],
        [-w[0][1], -w[1][1], g, h],
    ]


def spd_inverse(normal, block=16):
    pivots = 4
    count = normal.shape[0]
    lane = lax.broadcasted_iota(jnp.int32, (1, count), 1)
    sub = lax.broadcasted_iota(jnp.int32, (block, 1), 0)
    for first in range(0, count, block):
        panel = normal[first:first + block, :]
        for i in range(0, block, pivots):
            k = first + i
            cols = [jnp.broadcast_to(panel[:, k + m:k + m + 1], (block, count)) for m in range(pivots)]
            entry = [[jnp.broadcast_to(cols[n][i + m:i + m + 1, :], (8, count)) for n in range(pivots)] for m in range(pivots)]
            q = quad_inverse(entry)
            inside = jnp.logical_and(lane >= k, lane < k + pivots)
            rows = [
                jnp.where(inside, jnp.where(lane == k + m, 1.0, 0.0), jnp.broadcast_to(panel[i + m:i + m + 1, :], (8, count)))
                for m in range(pivots)
            ]
            new = [q[m][0] * rows[0] + (q[m][1] * rows[1] + (q[m][2] * rows[2] + q[m][3] * rows[3])) for m in range(pivots)]
            new = [jnp.concatenate([row] * (block // 8), axis=0) for row in new]
            panel = jnp.where(inside, 0.0, panel)
            for m in range(pivots):
                panel = panel - cols[m] * new[m]
            for m in range(pivots):
                panel = jnp.where(sub == i + m, new[m], panel)
        within = jnp.logical_and(lane >= first, lane < first + block)
        outer = jnp.dot(normal[:, first:first + block], panel, precision=HIGHEST, preferred_element_type=jnp.float32)
        rest = jnp.where(within, 0.0, normal) - outer
        above = [rest[:first]] if first > 0 else []
        below = [rest[first + block:]] if first + block < count else []
        normal = jnp.concatenate(above + [panel] + below, axis=0)
    return normal


def invert_kernel(mine_ref, theirs_ref, out_ref):
    core = lax.axis_index("wide") % CORES
    mine, theirs = mine_ref[...], theirs_ref[...]
    low = jnp.where(core == 0, mine, theirs)
    high = jnp.where(core == 0, theirs, mine)
    touched = jnp.concatenate([low, high], axis=0)
    count = touched.shape[0]
    row = lax.broadcasted_iota(jnp.int32, (count, count), 0)
    column = lax.broadcasted_iota(jnp.int32, (count, count), 1)
    capacitance = jnp.where(row == column, 1.0, 0.0) - touched
    normal = lax.dot_general(
        capacitance, capacitance, (((1,), (1,)), ((), ())), precision=HIGHEST, preferred_element_type=jnp.float32
    )
    out_ref[...] = jnp.dot(spd_inverse(normal), capacitance, precision=HIGHEST, preferred_element_type=jnp.float32)


def invert(mine, theirs):
    count = mine.shape[1]
    return pl.pallas_call(
        invert_kernel,
        out_shape=jax.ShapeDtypeStruct((count, count), jnp.float32),
        cost_estimate=pl.CostEstimate(flops=30_000_000, bytes_accessed=200_000, transcendentals=0),
        name="invert_capacitance",
    )(mine, theirs)


def update_kernel(column_ref, inverse_ref, *refs):
    narrow = len(refs) - 2 * XS - 3
    parts, refs = refs[:narrow], refs[narrow:]
    g_ref, mine, theirs, out_ref, left_ref = refs[0], refs[1:1 + XS], refs[1 + XS:1 + 2 * XS], refs[1 + 2 * XS], refs[2 + 2 * XS]
    half = mine[0].shape[0]
    step = pl.program_id(0)
    core = lax.axis_index("wide") % CORES

    @pl.when(step == 0)
    def _():
        response = parts[0][...]
        for part in parts[1:]:
            response = response + part[...]
        solved = lax.dot_general(
            response, inverse_ref[...], (((1,), (1,)), ((), ())), precision=HIGHEST, preferred_element_type=jnp.float32
        )
        low, high = solved[:, :half], solved[:, half:]
        s_mine = jnp.where(core == 0, low, high)
        s_theirs = jnp.where(core == 0, high, low)
        s_high, s_low = split(jnp.concatenate([s_mine, s_theirs], axis=1))
        left_ref[...] = jnp.concatenate([s_high, s_low, s_high], axis=1)

    for j in range(XS):
        @pl.when(step == j)
        def _():
            r_high, r_low = split(jnp.concatenate([mine[j][...], theirs[j][...]], axis=0))
            right = jnp.concatenate([r_high, r_high, r_low], axis=0)
            out_ref[...] = g_ref[...] + jnp.dot(left_ref[...], right, preferred_element_type=jnp.float32)


def update(gebhart, inverse, parts, mine, theirs, columns):
    rows, nodes = gebhart.shape
    half, width = mine[0].shape
    count = inverse.shape[0]
    piece = pl.BlockSpec((half, width), lambda i, col: (0, 0))
    block = pl.BlockSpec((rows, width), lambda i, col: (0, col[i]))
    part = pl.BlockSpec((rows, count), lambda i, col: (0, 0))
    return pl.pallas_call(
        update_kernel,
        out_shape=jax.ShapeDtypeStruct((rows, nodes), jnp.float32),
        grid_spec=pltpu.PrefetchScalarGridSpec(
            num_scalar_prefetch=1,
            grid=(XS,),
            in_specs=[pl.BlockSpec((count, count), lambda i, col: (0, 0))] + [part] * len(parts) + [block] + [piece] * (2 * XS),
            out_specs=block,
            scratch_shapes=[pltpu.VMEM((rows, 3 * count), jnp.bfloat16)],
        ),
        compiler_params=pltpu.CompilerParams(vmem_limit_bytes=60 * 1024 * 1024),
        name="update_rows",
    )(columns, inverse, *parts, gebhart, *mine, *theirs)


def body(wide, narrow, gebhart, change, moved_nodes):
    rows_local, width_local = gebhart.shape
    count = moved_nodes.shape[0]
    half = count // CORES
    zs = wide // (CORES * XS)
    width = width_local // XS
    group = half // zs
    me = lax.axis_index("wide")
    core = me % CORES
    x = (me // CORES) % XS
    z = me // (CORES * XS)

    def index(z, x, c):
        return (z * XS + x) * CORES + c

    places = [(z, x, c) for z in range(zs) for x in range(XS) for c in range(CORES)]
    swap = [(index(z, x, c), index(z, x, (c + 1) % CORES)) for z, x, c in places]
    shift_x = [[(index(z, x, c), index(z, (x + d) % XS, c)) for z, x, c in places] for d in range(XS)]
    shift_y = [[(i, (i + d) % narrow) for i in range(narrow)] for d in range(narrow)]
    x_groups = [[index(z, x, c) for x in range(XS)] for z in range(zs) for c in range(CORES)]
    z_groups = [[index(z, x, c) for z in range(zs)] for x in range(XS) for c in range(CORES)]

    owner = moved_nodes // rows_local
    owner_half = lax.dynamic_slice(owner, (core * half,), (half,))
    owner_core = owner_half % CORES
    owner_x = (owner_half // CORES) % XS
    owner_z = lax.dynamic_slice(owner_half // (CORES * XS), (z * group,), (group,))

    keep, send = pick(gebhart, moved_nodes, half, width)
    got = lax.ppermute(send, "wide", swap)

    partial_value = jnp.dot(gebhart, change, preferred_element_type=jnp.float32, precision=lax.Precision.HIGH)
    positions = me * rows_local + lax.broadcasted_iota(jnp.int32, (count, rows_local), 1)
    select = (moved_nodes[:, None] == positions).astype(jnp.float32)
    terms = jnp.dot(select, partial_value, preferred_element_type=jnp.float32, precision=HIGHEST)
    terms_mine = lax.dynamic_slice(terms, (core * half, 0), (half, count))
    terms_theirs = lax.dynamic_slice(terms, ((1 - core) * half, 0), (half, count))
    terms_chip = terms_mine + lax.ppermute(terms_theirs, "wide", swap)
    parts = [partial_value] + [lax.ppermute(partial_value, "narrow", shift_y[d]) for d in range(1, narrow)]

    rows_chip = jnp.where((owner_core == core)[None, :, None], keep, got)
    both = jnp.concatenate([rows_chip, jnp.broadcast_to(terms_chip[None], (XS, half, count))], axis=2)
    both = lax.all_to_all(both, "wide", 0, 0, axis_index_groups=x_groups)
    chosen = owner_x[None, :, None] == lax.broadcasted_iota(jnp.int32, (XS, 1, 1), 0)
    both = jnp.sum(jnp.where(chosen, both, 0.0), axis=0)

    both = lax.all_to_all(both.reshape(zs, group, width + count), "wide", 0, 0, axis_index_groups=z_groups)
    chosen = owner_z[None, :, None] == lax.broadcasted_iota(jnp.int32, (zs, 1, 1), 0)
    both = jnp.sum(jnp.where(chosen, both, 0.0), axis=0)
    both = lax.all_to_all(jnp.broadcast_to(both[None], (zs,) + both.shape), "wide", 0, 0, axis_index_groups=z_groups)
    both = both.reshape(half, width + count)

    touched_part = both[:, width:]
    touched = touched_part
    for d in range(1, narrow):
        touched = touched + lax.ppermute(touched_part, "narrow", shift_y[d])
    inverse = invert(touched, lax.ppermute(touched, "wide", swap))

    piece = both[:, :width]
    pieces = [piece] + [lax.ppermute(piece, "wide", shift_x[d]) for d in range(1, XS)]
    theirs = [lax.ppermute(p, "wide", swap) for p in pieces]
    columns = jnp.stack([(x - d) % XS for d in range(XS)]).astype(jnp.int32)
    return update(gebhart, inverse, parts, pieces, theirs, columns)


def solution(mesh):
    return jax.shard_map(
        functools.partial(body, mesh.shape["wide"], mesh.shape["narrow"]),
        mesh=mesh,
        in_specs=(P("wide", "narrow"), P("narrow", None), P()),
        out_specs=P("wide", "narrow"),
        check_vma=False,
    )
```

```python
import functools

import jax
import jax.numpy as jnp
from jax import lax
from jax.experimental import pallas as pl
from jax.experimental.pallas import tpu as pltpu
from jax.sharding import PartitionSpec as P

HIGHEST = lax.Precision.HIGHEST
CORES = 2
XS = 4
SLOTS = 8
PLANE = 32


def respond_kernel(moved_ref, lanes_ref, g_ref, change_ref, out_ref, pick_ref, table_ref, kept_ref, lines_ref, g_sem, c_sem):
    rows, count = out_ref.shape
    width = pick_ref.shape[2] - count
    chunks = g_sem.shape[0]
    block = kept_ref.shape[1] // chunks
    me = lax.axis_index("wide")
    first = me * rows

    copies = []
    for i in range(chunks):
        span = pl.ds(i * block, block)
        copies.append((
            pltpu.make_async_copy(g_ref.at[:, span], kept_ref.at[:, span], g_sem.at[i]),
            pltpu.make_async_copy(change_ref.at[span, :], lines_ref.at[span, :], c_sem.at[i]),
        ))
        for copy in copies[-1]:
            copy.start()

    lane = lax.broadcasted_iota(jnp.int32, (1, count), 1)
    node = lanes_ref[...]
    owned = jnp.logical_and(node >= first, node < first + rows)
    places = jnp.where(owned, lane, count).astype(jnp.float32)
    last = -1.0
    local = []
    for slot in range(SLOTS):
        last = jnp.min(jnp.where(places > last, places, float(count)))
        found = last < float(count)
        local.append(jnp.where(found, moved_ref[jnp.where(found, last, 0.0).astype(jnp.int32)] - first, 0))

    shift = rows.bit_length() - 1
    across = jnp.broadcast_to(lax.shift_right_logical(node, shift), (count, count)).astype(jnp.float32)
    down = across.T
    per_plane = float(CORES * XS)
    plane_across = jnp.floor(across / per_plane)
    plane_down = jnp.floor(down / per_plane)
    i = lax.broadcasted_iota(jnp.int32, (count, count), 0)
    j = lax.broadcasted_iota(jnp.int32, (count, count), 1)
    one = jnp.where(across == down, 1.0, 0.0)
    plane = jnp.where(plane_across == plane_down, 1.0, 0.0)
    slot = jnp.sum(jnp.where(j < i, one, 0.0), axis=1, keepdims=True)
    rank = jnp.sum(jnp.where(j < i, plane, 0.0), axis=1, keepdims=True)
    rank_across = jnp.sum(jnp.where(i < j, plane, 0.0), axis=0, keepdims=True)
    fits = jnp.where(jnp.logical_and(jnp.max(slot) < SLOTS, jnp.max(rank) < PLANE), 1, 0)
    inside = down - plane_down * per_plane
    x_down = jnp.floor(inside / float(CORES))
    core_down = inside - x_down * float(CORES)
    mine = jnp.where(core_down == (me % CORES).astype(jnp.float32), 0.0, float(XS * SLOTS))
    here = plane_down == (me // (CORES * XS)).astype(jnp.float32)
    match = jnp.logical_and(here, rank == j.astype(jnp.float32))
    source = jnp.sum(jnp.where(match, x_down * float(SLOTS) + jnp.minimum(slot, SLOTS - 1.0) + mine, 0.0), axis=0, keepdims=True)
    target = plane_across[:1] * float(PLANE) + jnp.minimum(rank_across, PLANE - 1.0)
    table_ref[0:1, :] = target.astype(jnp.int32)
    table_ref[1:2, :] = source.astype(jnp.int32)
    table_ref[2:8, :] = jnp.full((6, count), fits, jnp.int32)

    total = jnp.zeros((rows, count), jnp.float32)
    for i in range(chunks):
        for copy in copies[i]:
            copy.wait()
        g_high, g_low = split(kept_ref[:, i * block:(i + 1) * block])
        c_high, c_low = split(lines_ref[i * block:(i + 1) * block, :])
        wide_sum = jnp.dot(g_high, jnp.concatenate([c_high, c_low], axis=1), preferred_element_type=jnp.float32)
        low_sum = jnp.dot(g_low, c_high, preferred_element_type=jnp.float32)
        total = total + (wide_sum[:, :count] + (wide_sum[:, count:] + low_sum))
    out_ref[...] = total

    for slot in range(SLOTS):
        at = pl.ds(local[slot], 1)
        row = kept_ref[at, :]
        extra = out_ref[at, :]
        for q in range(XS):
            pick_ref[q, slot:slot + 1, :width] = row[:, q * width:(q + 1) * width]
            pick_ref[q, slot:slot + 1, width:] = extra


def respond(gebhart, change, moved_nodes):
    rows, nodes = gebhart.shape
    count = change.shape[1]
    chunks = 8
    vmem = pl.BlockSpec(memory_space=pltpu.VMEM)
    return pl.pallas_call(
        respond_kernel,
        out_shape=(
            jax.ShapeDtypeStruct((rows, count), jnp.float32),
            jax.ShapeDtypeStruct((XS, SLOTS, nodes // XS + count), jnp.float32),
            jax.ShapeDtypeStruct((8, count), jnp.int32),
        ),
        in_specs=[
            pl.BlockSpec(memory_space=pltpu.SMEM),
            vmem,
            pl.BlockSpec(memory_space=pl.ANY),
            pl.BlockSpec(memory_space=pl.ANY),
        ],
        out_specs=(vmem, vmem, vmem),
        scratch_shapes=[
            pltpu.VMEM((rows, nodes), jnp.float32),
            pltpu.VMEM((nodes, count), jnp.float32),
            pltpu.SemaphoreType.DMA((chunks,)),
            pltpu.SemaphoreType.DMA((chunks,)),
        ],
        compiler_params=pltpu.CompilerParams(vmem_limit_bytes=60 * 1024 * 1024),
        name="respond_and_pick",
    )(moved_nodes, moved_nodes.reshape(1, count), gebhart, change)


def plane_kernel(table_ref, own_ref, other_ref, out_ref, rows_ref):
    copies, plane, _ = out_ref.shape
    count = table_ref.shape[1]
    core = lax.axis_index("wide") % CORES
    width = own_ref.shape[1] - count
    part = width // CORES
    slots = own_ref.shape[0]
    for side, ref in ((0, own_ref), (1, other_ref)):
        value = ref[...]
        kept = jnp.where(core == 0, value[:, :part], value[:, part:width])
        rows_ref[side * slots:(side + 1) * slots, :part] = kept
        rows_ref[side * slots:(side + 1) * slots, part:] = value[:, width:]
    for i in range(plane):
        out_ref[0, i:i + 1, :] = rows_ref[pl.ds(table_ref[1, i], 1), :]
    value = out_ref[0]
    for copy in range(1, copies):
        out_ref[copy] = value


def plane_slots(table, own, other, planes):
    count = table.shape[1]
    slots, columns = own.shape
    columns = (columns - count) // CORES + count
    vmem = pl.BlockSpec(memory_space=pltpu.VMEM)
    return pl.pallas_call(
        plane_kernel,
        out_shape=jax.ShapeDtypeStruct((planes, PLANE, columns), jnp.float32),
        in_specs=[pl.BlockSpec(memory_space=pltpu.SMEM), vmem, vmem],
        out_specs=vmem,
        scratch_shapes=[pltpu.VMEM((2 * slots, columns), jnp.float32)],
        compiler_params=pltpu.CompilerParams(vmem_limit_bytes=16 * 1024 * 1024),
        name="plane_slots",
    )(table, own, other)


def order_kernel(table_ref, slots_ref, rows_ref, touched_ref):
    count, part = rows_ref.shape
    for k in range(count):
        row = slots_ref[pl.ds(table_ref[0, k], 1), :]
        rows_ref[k:k + 1, :] = row[:, :part]
        touched_ref[0, k:k + 1, :] = row[:, part:]
    touched = touched_ref[0]
    for copy in range(1, touched_ref.shape[0]):
        touched_ref[copy] = touched


def order(table, slots, receivers):
    count = table.shape[1]
    part = slots.shape[1] - count
    vmem = pl.BlockSpec(memory_space=pltpu.VMEM)
    return pl.pallas_call(
        order_kernel,
        out_shape=(jax.ShapeDtypeStruct((count, part), jnp.float32), jax.ShapeDtypeStruct((receivers, count, count), jnp.float32)),
        in_specs=[pl.BlockSpec(memory_space=pltpu.SMEM), vmem],
        out_specs=(vmem, vmem),
        compiler_params=pltpu.CompilerParams(vmem_limit_bytes=16 * 1024 * 1024),
        name="order_rows",
    )(table, slots)


def pick_kernel(moved_ref, g_ref, keep_ref, send_ref, sem):
    rows_local = g_ref.shape[0]
    quarters, half, width = keep_ref.shape
    me = lax.axis_index("wide")
    first = me * rows_local
    core = me % CORES

    def copy(local, target, row, q):
        return pltpu.make_async_copy(
            g_ref.at[pl.ds(local, 1), pl.ds(q * width, width)], target.at[q, pl.ds(row, 1), :], sem
        )

    total = 0
    for side in range(CORES):
        def start(row, found, side=side):
            local = moved_ref[side * half + row] - first
            owned = jnp.logical_and(local >= 0, local < rows_local)

            @pl.when(owned)
            def _():
                @pl.when(core == side)
                def _():
                    for q in range(quarters):
                        copy(local, keep_ref, row, q).start()

                @pl.when(core != side)
                def _():
                    for q in range(quarters):
                        copy(local, send_ref, row, q).start()

            return found + jnp.where(owned, 1, 0)

        total = lax.fori_loop(0, half, start, total, unroll=8)

    def wait(i, carry):
        for q in range(quarters):
            copy(0, keep_ref, 0, q).wait()
        return carry

    lax.fori_loop(0, total, wait, 0)


def pick(gebhart, moved_nodes, half, width):
    shape = jax.ShapeDtypeStruct((XS, half, width), jnp.float32)
    return pl.pallas_call(
        pick_kernel,
        out_shape=(shape, shape),
        in_specs=[pl.BlockSpec(memory_space=pltpu.SMEM), pl.BlockSpec(memory_space=pl.ANY)],
        out_specs=(pl.BlockSpec(memory_space=pl.ANY), pl.BlockSpec(memory_space=pl.ANY)),
        scratch_shapes=[pltpu.SemaphoreType.DMA],
        compiler_params=pltpu.CompilerParams(vmem_limit_bytes=60 * 1024 * 1024),
        name="pick_rows",
    )(moved_nodes, gebhart)


def split(value):
    high = value.astype(jnp.bfloat16)
    low = (value - high.astype(jnp.float32)).astype(jnp.bfloat16)
    return high, low


def pair_inverse(p, q, s):
    scale = 1.0 / (p * s - q * q)
    return s * scale, -q * scale, p * scale


def quad_inverse(e):
    a, b, c = pair_inverse(e[0][0], e[0][1], e[1][1])
    t = [[a * e[0][2] + b * e[1][2], a * e[0][3] + b * e[1][3]], [b * e[0][2] + c * e[1][2], b * e[0][3] + c * e[1][3]]]
    s22 = e[2][2] - (e[0][2] * t[0][0] + e[1][2] * t[1][0])
    s23 = e[2][3] - (e[0][2] * t[0][1] + e[1][2] * t[1][1])
    s33 = e[3][3] - (e[0][3] * t[0][1] + e[1][3] * t[1][1])
    f, g, h = pair_inverse(s22, s23, s33)
    w = [[t[0][0] * f + t[0][1] * g, t[0][0] * g + t[0][1] * h], [t[1][0] * f + t[1][1] * g, t[1][0] * g + t[1][1] * h]]
    i00 = a + w[0][0] * t[0][0] + w[0][1] * t[0][1]
    i01 = b + w[0][0] * t[1][0] + w[0][1] * t[1][1]
    i11 = c + w[1][0] * t[1][0] + w[1][1] * t[1][1]
    return [
        [i00, i01, -w[0][0], -w[0][1]],
        [i01, i11, -w[1][0], -w[1][1]],
        [-w[0][0], -w[1][0], f, g],
        [-w[0][1], -w[1][1], g, h],
    ]


def spd_inverse(normal, block=16):
    pivots = 4
    count = normal.shape[0]
    lane = lax.broadcasted_iota(jnp.int32, (1, count), 1)
    sub = lax.broadcasted_iota(jnp.int32, (block, 1), 0)
    for first in range(0, count, block):
        panel = normal[first:first + block, :]
        for i in range(0, block, pivots):
            k = first + i
            cols = [jnp.broadcast_to(panel[:, k + m:k + m + 1], (block, count)) for m in range(pivots)]
            entry = [[jnp.broadcast_to(cols[n][i + m:i + m + 1, :], (8, count)) for n in range(pivots)] for m in range(pivots)]
            q = quad_inverse(entry)
            inside = jnp.logical_and(lane >= k, lane < k + pivots)
            rows = [
                jnp.where(inside, jnp.where(lane == k + m, 1.0, 0.0), jnp.broadcast_to(panel[i + m:i + m + 1, :], (8, count)))
                for m in range(pivots)
            ]
            new = [q[m][0] * rows[0] + (q[m][1] * rows[1] + (q[m][2] * rows[2] + q[m][3] * rows[3])) for m in range(pivots)]
            new = [jnp.concatenate([row] * (block // 8), axis=0) for row in new]
            panel = jnp.where(inside, 0.0, panel)
            for m in range(pivots):
                panel = panel - cols[m] * new[m]
            for m in range(pivots):
                panel = jnp.where(sub == i + m, new[m], panel)
        within = jnp.logical_and(lane >= first, lane < first + block)
        outer = jnp.dot(normal[:, first:first + block], panel, precision=HIGHEST, preferred_element_type=jnp.float32)
        rest = jnp.where(within, 0.0, normal) - outer
        above = [rest[:first]] if first > 0 else []
        below = [rest[first + block:]] if first + block < count else []
        normal = jnp.concatenate(above + [panel] + below, axis=0)
    return normal


def invert_kernel(parts_ref, g_ref, out_ref, kept_ref, sem):
    copy = pltpu.make_async_copy(g_ref, kept_ref, sem)
    copy.start()
    touched = parts_ref[0]
    for i in range(1, parts_ref.shape[0]):
        touched = touched + parts_ref[i]
    count = touched.shape[0]
    row = lax.broadcasted_iota(jnp.int32, (count, count), 0)
    column = lax.broadcasted_iota(jnp.int32, (count, count), 1)
    capacitance = jnp.where(row == column, 1.0, 0.0) - touched
    normal = lax.dot_general(
        capacitance, capacitance, (((1,), (1,)), ((), ())), precision=HIGHEST, preferred_element_type=jnp.float32
    )
    out_ref[...] = jnp.dot(spd_inverse(normal), capacitance, precision=HIGHEST, preferred_element_type=jnp.float32)
    copy.wait()


def invert(parts, gebhart):
    vmem = pl.BlockSpec(memory_space=pltpu.VMEM)
    return pl.pallas_call(
        invert_kernel,
        out_shape=(jax.ShapeDtypeStruct(parts.shape[1:], jnp.float32), pltpu.VMEM(gebhart.shape, jnp.float32)),
        in_specs=[vmem, pl.BlockSpec(memory_space=pl.ANY)],
        out_specs=(vmem, vmem),
        scratch_shapes=[pltpu.SemaphoreType.DMA],
        cost_estimate=pl.CostEstimate(flops=30_000_000, bytes_accessed=200_000, transcendentals=0),
        compiler_params=pltpu.CompilerParams(vmem_limit_bytes=16 * 1024 * 1024),
        name="invert_capacitance",
    )(parts, gebhart)


def update_kernel(inverse_ref, g_ref, *refs):
    out_ref, buffer_ref, sem = refs[-3:]
    parts, pieces = refs[:-3 - 2 * XS], refs[-3 - 2 * XS:-3]
    me = lax.axis_index("wide")
    core = me % CORES
    x = (me // CORES) % XS
    part = pieces[0].shape[1]
    width = CORES * part
    response = parts[0][...]
    for ref in parts[1:]:
        response = response + ref[...]
    solved = lax.dot_general(
        response, inverse_ref[...], (((1,), (1,)), ((), ())), precision=HIGHEST, preferred_element_type=jnp.float32
    )
    s_high, s_low = split(solved)
    left = jnp.concatenate([s_high, s_low, s_high], axis=1)
    copies = []
    for d in range(XS):
        begin = lax.rem(x + (XS - d), XS) * width
        mine, theirs = pieces[d][...], pieces[XS + d][...]
        for side in range(CORES):
            r_high, r_low = split(jnp.where(core == side, mine, theirs))
            right = jnp.concatenate([r_high, r_high, r_low], axis=0)
            here = pl.ds(pl.multiple_of(begin + side * part, part), part)
            slot = d * CORES + side
            buffer_ref[slot] = g_ref[:, here] + jnp.dot(left, right, preferred_element_type=jnp.float32)
            copies.append(pltpu.make_async_copy(buffer_ref.at[slot], out_ref.at[:, here], sem.at[slot]))
            copies[slot].start()
    for copy in copies:
        copy.wait()


def update(kept, inverse, response, mine, theirs):
    rows, nodes = kept.shape
    part = mine[0].shape[1]
    vmem = pl.BlockSpec(memory_space=pltpu.VMEM)
    blocks = CORES * XS
    return pl.pallas_call(
        update_kernel,
        out_shape=jax.ShapeDtypeStruct((rows, nodes), jnp.float32),
        in_specs=[vmem] * (2 + len(response) + 2 * XS),
        out_specs=pl.BlockSpec(memory_space=pl.ANY),
        scratch_shapes=[pltpu.VMEM((blocks, rows, part), jnp.float32), pltpu.SemaphoreType.DMA((blocks,))],
        compiler_params=pltpu.CompilerParams(vmem_limit_bytes=20 * 1024 * 1024),
        name="update_rows",
    )(inverse, kept, *response, *mine, *theirs)


def body(wide, narrow, gebhart, change, moved_nodes):
    rows_local, width_local = gebhart.shape
    count = moved_nodes.shape[0]
    half = count // CORES
    zs = wide // (CORES * XS)
    width = width_local // XS
    group = half // zs
    me = lax.axis_index("wide")
    core = me % CORES
    x = (me // CORES) % XS
    z = me // (CORES * XS)

    def index(z, x, c):
        return (z * XS + x) * CORES + c

    places = [(z, x, c) for z in range(zs) for x in range(XS) for c in range(CORES)]
    swap = [(index(z, x, c), index(z, x, (c + 1) % CORES)) for z, x, c in places]
    shift_x = [[(index(z, x, c), index(z, (x + d) % XS, c)) for z, x, c in places] for d in range(XS)]
    shift_y = [[(i, (i + d) % narrow) for i in range(narrow)] for d in range(narrow)]
    x_groups = [[index(z, x, c) for x in range(XS)] for z in range(zs) for c in range(CORES)]
    z_groups = [[index(z, x, c) for z in range(zs)] for x in range(XS) for c in range(CORES)]

    part = width // CORES
    partial_value, picked, table = respond(gebhart, change, moved_nodes)

    def received(value):
        return [lax.ppermute(value, "narrow", shift_y[d]) for d in range(1, narrow)]

    def spread(gebhart, moved_nodes, partial_value, picked, table):
        own = lax.all_to_all(picked, "wide", 0, 0, axis_index_groups=x_groups).reshape(XS * SLOTS, width + count)
        other = lax.ppermute(own, "wide", swap)
        slots = plane_slots(table, own, other, zs)
        slots, partial_value = lax.optimization_barrier((slots, partial_value))
        parts = received(partial_value)
        slots = lax.all_to_all(slots, "wide", 0, 0, axis_index_groups=z_groups)
        return order(table, slots.reshape(zs * PLANE, part + count), narrow) + tuple(parts)

    def crowded(gebhart, moved_nodes, partial_value, picked, table):
        owner = moved_nodes // rows_local
        owner_half = lax.dynamic_slice(owner, (core * half,), (half,))
        owner_core = owner_half % CORES
        owner_x = (owner_half // CORES) % XS
        owner_z = lax.dynamic_slice(owner_half // (CORES * XS), (z * group,), (group,))

        keep, send = pick(gebhart, moved_nodes, half, width)
        got = lax.ppermute(send, "wide", swap)
        positions = me * rows_local + lax.broadcasted_iota(jnp.int32, (count, rows_local), 1)
        select = (moved_nodes[:, None] == positions).astype(jnp.float32)
        terms = jnp.dot(select, partial_value, preferred_element_type=jnp.float32, precision=HIGHEST)
        terms_mine = lax.dynamic_slice(terms, (core * half, 0), (half, count))
        terms_theirs = lax.dynamic_slice(terms, ((1 - core) * half, 0), (half, count))
        terms_chip = terms_mine + lax.ppermute(terms_theirs, "wide", swap)

        rows_chip = jnp.where((owner_core == core)[None, :, None], keep, got)
        both = jnp.concatenate([rows_chip, jnp.broadcast_to(terms_chip[None], (XS, half, count))], axis=2)
        both = lax.all_to_all(both, "wide", 0, 0, axis_index_groups=x_groups)
        chosen = owner_x[None, :, None] == lax.broadcasted_iota(jnp.int32, (XS, 1, 1), 0)
        both = jnp.sum(jnp.where(chosen, both, 0.0), axis=0)

        both = lax.all_to_all(both.reshape(zs, group, width + count), "wide", 0, 0, axis_index_groups=z_groups)
        chosen = owner_z[None, :, None] == lax.broadcasted_iota(jnp.int32, (zs, 1, 1), 0)
        both = jnp.sum(jnp.where(chosen, both, 0.0), axis=0)
        both = lax.all_to_all(jnp.broadcast_to(both[None], (zs,) + both.shape), "wide", 0, 0, axis_index_groups=z_groups)
        both = both.reshape(half, width + count)

        mine = jnp.concatenate([lax.dynamic_slice(both, (0, core * part), (half, part)), both[:, width:]], axis=1)
        theirs = jnp.concatenate([lax.dynamic_slice(both, (0, (1 - core) * part), (half, part)), both[:, width:]], axis=1)
        theirs = lax.ppermute(theirs, "wide", swap)
        both = jnp.where(core == 0, jnp.concatenate([mine, theirs]), jnp.concatenate([theirs, mine]))
        return (both[:, :part], jnp.broadcast_to(both[None, :, part:], (narrow, count, count))) + tuple(received(partial_value))

    mine, touched, *parts = lax.cond(table[2, 0] == 1, spread, crowded, gebhart, moved_nodes, partial_value, picked, table)
    inverse, kept = invert(lax.all_to_all(touched, "narrow", 0, 0), gebhart)
    pieces = [mine] + [lax.ppermute(mine, "wide", shift_x[d]) for d in range(1, XS)]
    pieces, inverse = lax.optimization_barrier((pieces, inverse))
    theirs = [lax.ppermute(piece, "wide", swap) for piece in pieces]
    return update(kept, inverse, [partial_value] + parts, pieces, theirs)


def solution(mesh):
    return jax.shard_map(
        functools.partial(body, mesh.shape["wide"], mesh.shape["narrow"]),
        mesh=mesh,
        in_specs=(P("wide", "narrow"), P("narrow", None), P()),
        out_specs=P("wide", "narrow"),
        check_vma=False,
    )
```

```python
import functools

import jax
import jax.numpy as jnp
from jax import lax
from jax.experimental import pallas as pl
from jax.experimental.pallas import tpu as pltpu
from jax.sharding import PartitionSpec as P

HIGHEST = lax.Precision.HIGHEST
CORES = 2
XS = 4
SLOTS = 8
PLANE = 32


def pick_kernel(lanes_ref, g_ref, change_ref, *refs):
    pick_refs, table_ref, line_ref, lines_ref, halves_ref, row_sem, sem = refs[:XS], *refs[XS:]
    nodes, count = lines_ref.shape
    rows = g_ref.shape[0]
    width = nodes // XS
    chunks = sem.shape[0]
    block = nodes // chunks
    me = lax.axis_index("wide")
    first = me * rows
    x = (me // CORES) % XS

    copies = []
    for i in range(chunks):
        span = pl.ds(i * block, block)
        copies.append(pltpu.make_async_copy(change_ref.at[span, :], lines_ref.at[span, :], sem.at[i]))
        copies[i].start()

    node_across = jnp.broadcast_to(lanes_ref[...].astype(jnp.float32), (count, count))
    node_down = node_across.T
    across = jnp.floor(node_across / float(rows))
    down = jnp.floor(node_down / float(rows))
    i = lax.broadcasted_iota(jnp.int32, (count, count), 0)
    j = lax.broadcasted_iota(jnp.int32, (count, count), 1)
    one = jnp.where(across == down, 1.0, 0.0)
    slot = jnp.sum(jnp.where(j < i, one, 0.0), axis=1, keepdims=True)
    match = jnp.logical_and(down == me.astype(jnp.float32), slot == j.astype(jnp.float32))
    local = jnp.sum(jnp.where(match, node_down - first.astype(jnp.float32), 0.0), axis=0, keepdims=True).astype(jnp.int32)
    picks = []
    for s in range(SLOTS):
        picks.append(pltpu.make_async_copy(g_ref.at[pl.ds(local[0, s], 1), :], line_ref.at[pl.ds(s, 1), :], row_sem.at[s]))
        picks[s].start()

    per_plane = float(CORES * XS)
    plane_across = jnp.floor(across / per_plane)
    plane_down = jnp.floor(down / per_plane)
    plane = jnp.where(plane_across == plane_down, 1.0, 0.0)
    rank = jnp.sum(jnp.where(j < i, plane, 0.0), axis=1, keepdims=True)
    rank_across = jnp.sum(jnp.where(i < j, plane, 0.0), axis=0, keepdims=True)
    fits = jnp.where(jnp.logical_and(jnp.max(slot) < SLOTS, jnp.max(rank) < PLANE), 1, 0)
    inside = down - plane_down * per_plane
    x_down = jnp.floor(inside / float(CORES))
    core_down = inside - x_down * float(CORES)
    behind = x.astype(jnp.float32) - x_down
    behind = jnp.where(behind < 0, behind + float(XS), behind)
    side = jnp.where(core_down == (me % CORES).astype(jnp.float32), 0.0, float(XS * SLOTS))
    here = plane_down == (me // (CORES * XS)).astype(jnp.float32)
    match = jnp.logical_and(here, rank == j.astype(jnp.float32))
    source = jnp.sum(jnp.where(match, behind * float(SLOTS) + jnp.minimum(slot, SLOTS - 1.0) + side, 0.0), axis=0, keepdims=True)
    target = plane_across[:1] * float(PLANE) + jnp.minimum(rank_across, PLANE - 1.0)
    table_ref[0:1, :] = target.astype(jnp.int32)
    table_ref[1:2, :] = source.astype(jnp.int32)
    table_ref[2:8, :] = jnp.full((6, count), fits, jnp.int32)

    for i in range(chunks):
        span = pl.ds(i * block, block)
        copies[i].wait()
        c_high, c_low = split(lines_ref[span, :])
        halves_ref[span, :count] = c_high
        halves_ref[span, count:] = c_low
    for pick in picks:
        pick.wait()
    r_high, r_low = split(line_ref[...])
    both = jnp.dot(jnp.concatenate([r_high, r_low], axis=0), halves_ref[...], preferred_element_type=jnp.float32)
    terms = both[:SLOTS, :count] + (both[:SLOTS, count:] + both[SLOTS:, :count])
    for d in range(XS):
        quarter = pl.ds(pl.multiple_of(lax.rem(x + d, XS) * width, width), width)
        pick_refs[d][:, :width] = line_ref[:, quarter]
        pick_refs[d][:, width:] = terms


def pick_slots(gebhart, change, moved_nodes):
    nodes, count = change.shape
    chunks = 4
    vmem = pl.BlockSpec(memory_space=pltpu.VMEM)
    hbm = pl.BlockSpec(memory_space=pl.ANY)
    *picked, table = pl.pallas_call(
        pick_kernel,
        out_shape=(jax.ShapeDtypeStruct((SLOTS, nodes // XS + count), jnp.float32),) * XS
        + (jax.ShapeDtypeStruct((8, count), jnp.int32),),
        in_specs=[vmem, hbm, hbm],
        out_specs=(vmem,) * (XS + 1),
        scratch_shapes=[
            pltpu.VMEM((SLOTS, nodes), jnp.float32),
            pltpu.VMEM((nodes, count), jnp.float32),
            pltpu.VMEM((nodes, 2 * count), jnp.bfloat16),
            pltpu.SemaphoreType.DMA((SLOTS,)),
            pltpu.SemaphoreType.DMA((chunks,)),
        ],
        compiler_params=pltpu.CompilerParams(vmem_limit_bytes=60 * 1024 * 1024),
        name="pick_slots",
    )(moved_nodes.reshape(1, count), gebhart, change)
    return picked, table


def respond_kernel(token_ref, g_ref, change_ref, out_ref, kept_ref, lines_ref, g_sem, c_sem):
    rows, count = out_ref.shape
    chunks = g_sem.shape[0]
    block = kept_ref.shape[1] // chunks
    copies = []
    for i in range(chunks):
        span = pl.ds(i * block, block)
        copies.append((
            pltpu.make_async_copy(g_ref.at[:, span], kept_ref.at[:, span], g_sem.at[i]),
            pltpu.make_async_copy(change_ref.at[span, :], lines_ref.at[span, :], c_sem.at[i]),
        ))
        for copy in copies[-1]:
            copy.start()
    total = jnp.zeros((rows, count), jnp.float32)
    for i in range(chunks):
        for copy in copies[i]:
            copy.wait()
        g_high, g_low = split(kept_ref[:, i * block:(i + 1) * block])
        c_high, c_low = split(lines_ref[i * block:(i + 1) * block, :])
        wide_sum = jnp.dot(g_high, jnp.concatenate([c_high, c_low], axis=1), preferred_element_type=jnp.float32)
        low_sum = jnp.dot(g_low, c_high, preferred_element_type=jnp.float32)
        total = total + (wide_sum[:, :count] + (wide_sum[:, count:] + low_sum))
    out_ref[...] = total


def respond(token, gebhart, change):
    rows, nodes = gebhart.shape
    count = change.shape[1]
    chunks = 8
    vmem = pl.BlockSpec(memory_space=pltpu.VMEM)
    hbm = pl.BlockSpec(memory_space=pl.ANY)
    return pl.pallas_call(
        respond_kernel,
        out_shape=jax.ShapeDtypeStruct((rows, count), jnp.float32),
        in_specs=[vmem, hbm, hbm],
        out_specs=vmem,
        scratch_shapes=[
            pltpu.VMEM((rows, nodes), jnp.float32),
            pltpu.VMEM((nodes, count), jnp.float32),
            pltpu.SemaphoreType.DMA((chunks,)),
            pltpu.SemaphoreType.DMA((chunks,)),
        ],
        cost_estimate=pl.CostEstimate(flops=800_000_000, bytes_accessed=8_000_000, transcendentals=0),
        compiler_params=pltpu.CompilerParams(vmem_limit_bytes=24 * 1024 * 1024),
        name="respond",
    )(token, gebhart, change)


def plane_kernel(table_ref, *refs):
    slots_refs, out_ref, rows_ref = refs[:-2], refs[-2], refs[-1]
    copies, plane, columns = out_ref.shape
    count = table_ref.shape[1]
    core = lax.axis_index("wide") % CORES
    part = columns - count
    width = CORES * part
    for i, ref in enumerate(slots_refs):
        value = ref[...]
        here = slice(i * SLOTS, (i + 1) * SLOTS)
        rows_ref[here, :part] = jnp.where(core == 0, value[:, :part], value[:, part:width])
        rows_ref[here, part:] = value[:, width:]
    for i in range(plane):
        out_ref[0, i:i + 1, :] = rows_ref[pl.ds(table_ref[1, i], 1), :]
    value = out_ref[0]
    for copy in range(1, copies):
        out_ref[copy] = value


def plane_slots(table, slots, planes):
    count = table.shape[1]
    columns = (slots[0].shape[1] - count) // CORES + count
    vmem = pl.BlockSpec(memory_space=pltpu.VMEM)
    return pl.pallas_call(
        plane_kernel,
        out_shape=jax.ShapeDtypeStruct((planes, PLANE, columns), jnp.float32),
        in_specs=[pl.BlockSpec(memory_space=pltpu.SMEM)] + [vmem] * len(slots),
        out_specs=vmem,
        scratch_shapes=[pltpu.VMEM((len(slots) * SLOTS, columns), jnp.float32)],
        compiler_params=pltpu.CompilerParams(vmem_limit_bytes=16 * 1024 * 1024),
        name="plane_slots",
    )(table, *slots)


def order_kernel(table_ref, slots_ref, rows_ref, touched_ref):
    copies, count, part = rows_ref.shape
    for k in range(count):
        row = slots_ref[pl.ds(table_ref[0, k], 1), :]
        rows_ref[0, k:k + 1, :] = row[:, :part]
        touched_ref[k:k + 1, :] = row[:, part:]
    rows = rows_ref[0]
    for copy in range(1, copies):
        rows_ref[copy] = rows


def order(table, slots):
    count = table.shape[1]
    part = slots.shape[1] - count
    vmem = pl.BlockSpec(memory_space=pltpu.VMEM)
    return pl.pallas_call(
        order_kernel,
        out_shape=(jax.ShapeDtypeStruct((XS, count, part), jnp.float32), jax.ShapeDtypeStruct((count, count), jnp.float32)),
        in_specs=[pl.BlockSpec(memory_space=pltpu.SMEM), vmem],
        out_specs=(vmem, vmem),
        compiler_params=pltpu.CompilerParams(vmem_limit_bytes=16 * 1024 * 1024),
        name="order_rows",
    )(table, slots)


def pick_all_kernel(moved_ref, g_ref, keep_ref, send_ref, sem):
    rows_local = g_ref.shape[0]
    quarters, half, width = keep_ref.shape
    me = lax.axis_index("wide")
    first = me * rows_local
    core = me % CORES

    def copy(local, target, row, q):
        return pltpu.make_async_copy(
            g_ref.at[pl.ds(local, 1), pl.ds(q * width, width)], target.at[q, pl.ds(row, 1), :], sem
        )

    total = 0
    for side in range(CORES):
        def start(row, found, side=side):
            local = moved_ref[side * half + row] - first
            owned = jnp.logical_and(local >= 0, local < rows_local)

            @pl.when(owned)
            def _():
                @pl.when(core == side)
                def _():
                    for q in range(quarters):
                        copy(local, keep_ref, row, q).start()

                @pl.when(core != side)
                def _():
                    for q in range(quarters):
                        copy(local, send_ref, row, q).start()

            return found + jnp.where(owned, 1, 0)

        total = lax.fori_loop(0, half, start, total, unroll=8)

    def wait(i, carry):
        for q in range(quarters):
            copy(0, keep_ref, 0, q).wait()
        return carry

    lax.fori_loop(0, total, wait, 0)


def pick_all(gebhart, moved_nodes, half, width):
    shape = jax.ShapeDtypeStruct((XS, half, width), jnp.float32)
    return pl.pallas_call(
        pick_all_kernel,
        out_shape=(shape, shape),
        in_specs=[pl.BlockSpec(memory_space=pltpu.SMEM), pl.BlockSpec(memory_space=pl.ANY)],
        out_specs=(pl.BlockSpec(memory_space=pl.ANY), pl.BlockSpec(memory_space=pl.ANY)),
        scratch_shapes=[pltpu.SemaphoreType.DMA],
        compiler_params=pltpu.CompilerParams(vmem_limit_bytes=60 * 1024 * 1024),
        name="pick_rows",
    )(moved_nodes, gebhart)


def split(value):
    high = value.astype(jnp.bfloat16)
    low = (value - high.astype(jnp.float32)).astype(jnp.bfloat16)
    return high, low


def pair_inverse(p, q, s):
    scale = 1.0 / (p * s - q * q)
    return s * scale, -q * scale, p * scale


def quad_inverse(e):
    a, b, c = pair_inverse(e[0][0], e[0][1], e[1][1])
    t = [[a * e[0][2] + b * e[1][2], a * e[0][3] + b * e[1][3]], [b * e[0][2] + c * e[1][2], b * e[0][3] + c * e[1][3]]]
    s22 = e[2][2] - (e[0][2] * t[0][0] + e[1][2] * t[1][0])
    s23 = e[2][3] - (e[0][2] * t[0][1] + e[1][2] * t[1][1])
    s33 = e[3][3] - (e[0][3] * t[0][1] + e[1][3] * t[1][1])
    f, g, h = pair_inverse(s22, s23, s33)
    w = [[t[0][0] * f + t[0][1] * g, t[0][0] * g + t[0][1] * h], [t[1][0] * f + t[1][1] * g, t[1][0] * g + t[1][1] * h]]
    i00 = a + w[0][0] * t[0][0] + w[0][1] * t[0][1]
    i01 = b + w[0][0] * t[1][0] + w[0][1] * t[1][1]
    i11 = c + w[1][0] * t[1][0] + w[1][1] * t[1][1]
    return [
        [i00, i01, -w[0][0], -w[0][1]],
        [i01, i11, -w[1][0], -w[1][1]],
        [-w[0][0], -w[1][0], f, g],
        [-w[0][1], -w[1][1], g, h],
    ]


def spd_inverse(normal, block=16):
    pivots = 4
    count = normal.shape[0]
    lane = lax.broadcasted_iota(jnp.int32, (1, count), 1)
    sub = lax.broadcasted_iota(jnp.int32, (block, 1), 0)
    for first in range(0, count, block):
        panel = normal[first:first + block, :]
        for i in range(0, block, pivots):
            k = first + i
            cols = [jnp.broadcast_to(panel[:, k + m:k + m + 1], (block, count)) for m in range(pivots)]
            entry = [[jnp.broadcast_to(cols[n][i + m:i + m + 1, :], (8, count)) for n in range(pivots)] for m in range(pivots)]
            q = quad_inverse(entry)
            inside = jnp.logical_and(lane >= k, lane < k + pivots)
            rows = [
                jnp.where(inside, jnp.where(lane == k + m, 1.0, 0.0), jnp.broadcast_to(panel[i + m:i + m + 1, :], (8, count)))
                for m in range(pivots)
            ]
            new = [q[m][0] * rows[0] + (q[m][1] * rows[1] + (q[m][2] * rows[2] + q[m][3] * rows[3])) for m in range(pivots)]
            new = [jnp.concatenate([row] * (block // 8), axis=0) for row in new]
            panel = jnp.where(inside, 0.0, panel)
            for m in range(pivots):
                panel = panel - cols[m] * new[m]
            for m in range(pivots):
                panel = jnp.where(sub == i + m, new[m], panel)
        within = jnp.logical_and(lane >= first, lane < first + block)
        outer = jnp.dot(normal[:, first:first + block], panel, precision=HIGHEST, preferred_element_type=jnp.float32)
        rest = jnp.where(within, 0.0, normal) - outer
        above = [rest[:first]] if first > 0 else []
        below = [rest[first + block:]] if first + block < count else []
        normal = jnp.concatenate(above + [panel] + below, axis=0)
    return normal


def invert_kernel(*refs):
    out_ref = refs[-1]
    touched = refs[0][...]
    for ref in refs[1:-1]:
        touched = touched + ref[...]
    count = touched.shape[0]
    row = lax.broadcasted_iota(jnp.int32, (count, count), 0)
    column = lax.broadcasted_iota(jnp.int32, (count, count), 1)
    capacitance = jnp.where(row == column, 1.0, 0.0) - touched
    normal = lax.dot_general(
        capacitance, capacitance, (((1,), (1,)), ((), ())), precision=HIGHEST, preferred_element_type=jnp.float32
    )
    out_ref[...] = jnp.dot(spd_inverse(normal), capacitance, precision=HIGHEST, preferred_element_type=jnp.float32)


def invert(parts):
    vmem = pl.BlockSpec(memory_space=pltpu.VMEM)
    return pl.pallas_call(
        invert_kernel,
        out_shape=jax.ShapeDtypeStruct(parts[0].shape, jnp.float32),
        in_specs=[vmem] * len(parts),
        out_specs=vmem,
        cost_estimate=pl.CostEstimate(flops=2_000_000_000, bytes_accessed=8_000_000, transcendentals=0),
        compiler_params=pltpu.CompilerParams(vmem_limit_bytes=16 * 1024 * 1024),
        name="invert_capacitance",
    )(*parts)


def places(core, part):
    return [pl.ds(pl.multiple_of((q * CORES + core) * part, part), part) for q in range(XS)]


def write_blocks(left, blocks, ready, pieces_ref, out_ref, buffer_ref, sem, core):
    copies = []
    for q, here in enumerate(places(core, pieces_ref.shape[2])):
        r_high, r_low = split(pieces_ref[q])
        right = jnp.concatenate([r_high, r_high, r_low], axis=0)
        change = jnp.dot(left, right, preferred_element_type=jnp.float32)
        if ready is not None:
            ready[q].wait()
        buffer_ref[q] = blocks[q] + change
        copies.append(pltpu.make_async_copy(buffer_ref.at[q], out_ref.at[:, here], sem.at[q]))
        copies[q].start()
    for copy in copies:
        copy.wait()


def update_own_kernel(inverse_ref, g_ref, pieces_ref, *refs):
    out_ref, left_ref, other_ref, own_ref, buffer_ref, own_sem, other_sem, sem = refs[-8:]
    core = lax.axis_index("wide") % CORES
    part = pieces_ref.shape[2]
    ready = []
    for q, here in enumerate(places(core, part)):
        ready.append(pltpu.make_async_copy(g_ref.at[:, here], own_ref.at[q], own_sem.at[q]))
        ready[q].start()
    later = []
    for q, here in enumerate(places(1 - core, part)):
        later.append(pltpu.make_async_copy(g_ref.at[:, here], other_ref.at[q], other_sem.at[q]))
        later[q].start()
    response = refs[0][...]
    for ref in refs[1:-8]:
        response = response + ref[...]
    solved = lax.dot_general(
        response, inverse_ref[...], (((1,), (1,)), ((), ())), precision=HIGHEST, preferred_element_type=jnp.float32
    )
    s_high, s_low = split(solved)
    left = jnp.concatenate([s_high, s_low, s_high], axis=1)
    left_ref[...] = left
    write_blocks(left, own_ref, ready, pieces_ref, out_ref, buffer_ref, sem, core)
    for copy in later:
        copy.wait()


def update_other_kernel(left_ref, blocks_ref, pieces_ref, before_ref, out_ref, buffer_ref, sem):
    write_blocks(left_ref[...], blocks_ref, None, pieces_ref, out_ref, buffer_ref, sem, 1 - lax.axis_index("wide") % CORES)


def update(gebhart, inverse, response, pieces, swapped):
    rows, nodes = gebhart.shape
    count, part = pieces.shape[1:]
    vmem = pl.BlockSpec(memory_space=pltpu.VMEM)
    hbm = pl.BlockSpec(memory_space=pl.ANY)
    whole = jax.ShapeDtypeStruct((rows, nodes), jnp.float32)
    blocks = pltpu.VMEM((XS, rows, part), jnp.float32)
    sems = pltpu.SemaphoreType.DMA((XS,))
    own, left, other = pl.pallas_call(
        update_own_kernel,
        out_shape=(whole, jax.ShapeDtypeStruct((rows, 3 * count), jnp.bfloat16), blocks),
        in_specs=[vmem, hbm] + [vmem] * (1 + len(response)),
        out_specs=(hbm, vmem, vmem),
        scratch_shapes=[blocks, blocks, sems, sems, sems],
        cost_estimate=pl.CostEstimate(flops=1_000_000_000, bytes_accessed=6_000_000, transcendentals=0),
        compiler_params=pltpu.CompilerParams(vmem_limit_bytes=20 * 1024 * 1024),
        name="update_own",
    )(inverse, gebhart, pieces, *response)
    return pl.pallas_call(
        update_other_kernel,
        out_shape=whole,
        in_specs=[vmem, vmem, vmem, hbm],
        out_specs=hbm,
        scratch_shapes=[blocks, sems],
        input_output_aliases={3: 0},
        compiler_params=pltpu.CompilerParams(vmem_limit_bytes=20 * 1024 * 1024),
        name="update_other",
    )(left, other, swapped, own)


def body(wide, narrow, gebhart, change, moved_nodes):
    rows_local, width_local = gebhart.shape
    count = moved_nodes.shape[0]
    half = count // CORES
    zs = wide // (CORES * XS)
    width = width_local // XS
    group = half // zs
    me = lax.axis_index("wide")
    core = me % CORES
    x = (me // CORES) % XS
    z = me // (CORES * XS)

    def index(z, x, c):
        return (z * XS + x) * CORES + c

    places = [(z, x, c) for z in range(zs) for x in range(XS) for c in range(CORES)]
    swap = [(index(z, x, c), index(z, x, (c + 1) % CORES)) for z, x, c in places]
    shift_x = [[(index(z, x, c), index(z, (x + d) % XS, c)) for z, x, c in places] for d in range(XS)]
    shift_y = [[(i, (i + d) % narrow) for i in range(narrow)] for d in range(narrow)]
    x_groups = [[index(z, x, c) for x in range(XS)] for z in range(zs) for c in range(CORES)]
    z_groups = [[index(z, x, c) for z in range(zs)] for x in range(XS) for c in range(CORES)]

    part = width // CORES
    picked, table = pick_slots(gebhart, change, moved_nodes)

    def received(value):
        return [lax.ppermute(value, "narrow", shift_y[d]) for d in range(1, narrow)]

    def finish(rows, touched, response, gebhart):
        pieces = lax.all_to_all(rows, "wide", 0, 0, axis_index_groups=x_groups)
        inverse = invert([touched] + received(touched))
        pieces, inverse = lax.optimization_barrier((pieces, inverse))
        return update(gebhart, inverse, response, pieces, lax.ppermute(pieces, "wide", swap))

    def spread(gebhart, change, moved_nodes, picked, table):
        own = [picked[0]] + [lax.ppermute(picked[d], "wide", shift_x[d]) for d in range(1, XS)]
        other = [lax.ppermute(slots, "wide", swap) for slots in own]
        slots = plane_slots(table, own + other, zs)
        slots, token = lax.optimization_barrier((slots, table))
        partial_value = respond(token, gebhart, change)
        response = [partial_value] + received(partial_value)
        slots = lax.all_to_all(slots, "wide", 0, 0, axis_index_groups=z_groups)
        slots, response = lax.optimization_barrier((slots, response))
        rows, touched = order(table, slots.reshape(zs * PLANE, part + count))
        return finish(rows, touched, response, gebhart)

    def crowded(gebhart, change, moved_nodes, picked, table):
        partial_value = respond(table, gebhart, change)
        owner = moved_nodes // rows_local
        owner_half = lax.dynamic_slice(owner, (core * half,), (half,))
        owner_core = owner_half % CORES
        owner_x = (owner_half // CORES) % XS
        owner_z = lax.dynamic_slice(owner_half // (CORES * XS), (z * group,), (group,))

        keep, send = pick_all(gebhart, moved_nodes, half, width)
        got = lax.ppermute(send, "wide", swap)
        positions = me * rows_local + lax.broadcasted_iota(jnp.int32, (count, rows_local), 1)
        select = (moved_nodes[:, None] == positions).astype(jnp.float32)
        terms = jnp.dot(select, partial_value, preferred_element_type=jnp.float32, precision=HIGHEST)
        terms_mine = lax.dynamic_slice(terms, (core * half, 0), (half, count))
        terms_theirs = lax.dynamic_slice(terms, ((1 - core) * half, 0), (half, count))
        terms_chip = terms_mine + lax.ppermute(terms_theirs, "wide", swap)

        rows_chip = jnp.where((owner_core == core)[None, :, None], keep, got)
        both = jnp.concatenate([rows_chip, jnp.broadcast_to(terms_chip[None], (XS, half, count))], axis=2)
        both = lax.all_to_all(both, "wide", 0, 0, axis_index_groups=x_groups)
        chosen = owner_x[None, :, None] == lax.broadcasted_iota(jnp.int32, (XS, 1, 1), 0)
        both = jnp.sum(jnp.where(chosen, both, 0.0), axis=0)

        both = lax.all_to_all(both.reshape(zs, group, width + count), "wide", 0, 0, axis_index_groups=z_groups)
        chosen = owner_z[None, :, None] == lax.broadcasted_iota(jnp.int32, (zs, 1, 1), 0)
        both = jnp.sum(jnp.where(chosen, both, 0.0), axis=0)
        both = lax.all_to_all(jnp.broadcast_to(both[None], (zs,) + both.shape), "wide", 0, 0, axis_index_groups=z_groups)
        both = both.reshape(half, width + count)

        mine = jnp.concatenate([lax.dynamic_slice(both, (0, core * part), (half, part)), both[:, width:]], axis=1)
        theirs = jnp.concatenate([lax.dynamic_slice(both, (0, (1 - core) * part), (half, part)), both[:, width:]], axis=1)
        theirs = lax.ppermute(theirs, "wide", swap)
        both = jnp.where(core == 0, jnp.concatenate([mine, theirs]), jnp.concatenate([theirs, mine]))
        rows = jnp.broadcast_to(both[None, :, :part], (XS, count, part))
        return finish(rows, both[:, part:], [partial_value] + received(partial_value), gebhart)

    return lax.cond(table[2, 0] == 1, spread, crowded, gebhart, change, moved_nodes, picked, table)


def solution(mesh):
    return jax.shard_map(
        functools.partial(body, mesh.shape["wide"], mesh.shape["narrow"]),
        mesh=mesh,
        in_specs=(P("wide", "narrow"), P("narrow", None), P()),
        out_specs=P("wide", "narrow"),
        check_vma=False,
    )
```

```python
import functools

import jax
import jax.numpy as jnp
from jax import lax
from jax.experimental import pallas as pl
from jax.experimental.pallas import tpu as pltpu
from jax.sharding import PartitionSpec as P

HIGHEST = lax.Precision.HIGHEST
CORES = 2
XS = 4
SLOTS = 16
PLANES = (24, 32)


def pick_kernel(lanes_ref, g_ref, change_ref, *refs):
    pick_refs, table_ref, line_ref, lines_ref, halves_ref, row_sem, sem = refs[:XS], *refs[XS:]
    nodes, count = lines_ref.shape
    rows = g_ref.shape[0]
    width = nodes // XS
    chunks = sem.shape[0]
    block = nodes // chunks
    me = lax.axis_index("wide")
    first = me * rows
    x = (me // CORES) % XS

    copies = []
    for i in range(chunks):
        span = pl.ds(i * block, block)
        copies.append(pltpu.make_async_copy(change_ref.at[span, :], lines_ref.at[span, :], sem.at[i]))
        copies[i].start()

    node_across = jnp.broadcast_to(lanes_ref[...].astype(jnp.float32), (count, count))
    node_down = node_across.T
    across = jnp.floor(node_across / float(rows))
    down = jnp.floor(node_down / float(rows))
    i = lax.broadcasted_iota(jnp.int32, (count, count), 0)
    j = lax.broadcasted_iota(jnp.int32, (count, count), 1)
    one = jnp.where(across == down, 1.0, 0.0)
    slot = jnp.sum(jnp.where(j < i, one, 0.0), axis=1, keepdims=True)
    match = jnp.logical_and(down == me.astype(jnp.float32), slot == j.astype(jnp.float32))
    local = jnp.sum(jnp.where(match, node_down - first.astype(jnp.float32), 0.0), axis=0, keepdims=True).astype(jnp.int32)
    picks = []
    for s in range(SLOTS):
        picks.append(pltpu.make_async_copy(g_ref.at[pl.ds(local[0, s], 1), :], line_ref.at[pl.ds(s, 1), :], row_sem.at[s]))
        picks[s].start()

    per_plane = float(CORES * XS)
    plane_across = jnp.floor(across / per_plane)
    plane_down = jnp.floor(down / per_plane)
    plane = jnp.where(plane_across == plane_down, 1.0, 0.0)
    rank = jnp.sum(jnp.where(j < i, plane, 0.0), axis=1, keepdims=True)
    rank_across = jnp.sum(jnp.where(i < j, plane, 0.0), axis=0, keepdims=True)
    most = jnp.max(rank)
    path = len(PLANES)
    room = float(PLANES[-1])
    for choice in reversed(range(len(PLANES))):
        path = jnp.where(most < PLANES[choice], choice, path)
        room = jnp.where(most < PLANES[choice], float(PLANES[choice]), room)
    path = jnp.where(jnp.max(slot) < SLOTS, path, len(PLANES))
    inside = down - plane_down * per_plane
    x_down = jnp.floor(inside / float(CORES))
    core_down = inside - x_down * float(CORES)
    behind = x.astype(jnp.float32) - x_down
    behind = jnp.where(behind < 0, behind + float(XS), behind)
    side = jnp.where(core_down == (me % CORES).astype(jnp.float32), 0.0, float(XS * SLOTS))
    here = plane_down == (me // (CORES * XS)).astype(jnp.float32)
    match = jnp.logical_and(here, rank == j.astype(jnp.float32))
    source = jnp.sum(jnp.where(match, behind * float(SLOTS) + jnp.minimum(slot, SLOTS - 1.0) + side, 0.0), axis=0, keepdims=True)
    target = plane_across[:1] * room + jnp.minimum(rank_across, room - 1.0)
    table_ref[0:1, :] = target.astype(jnp.int32)
    table_ref[1:2, :] = source.astype(jnp.int32)
    table_ref[2:8, :] = jnp.full((6, count), path, jnp.int32)

    for i in range(chunks):
        span = pl.ds(i * block, block)
        copies[i].wait()
        c_high, c_low = split(lines_ref[span, :])
        halves_ref[span, :count] = c_high
        halves_ref[span, count:] = c_low
    for pick in picks:
        pick.wait()
    r_high, r_low = split(line_ref[...])
    both = jnp.dot(jnp.concatenate([r_high, r_low], axis=0), halves_ref[...], preferred_element_type=jnp.float32)
    terms = both[:SLOTS, :count] + (both[:SLOTS, count:] + both[SLOTS:, :count])
    for d in range(XS):
        quarter = pl.ds(pl.multiple_of(lax.rem(x + d, XS) * width, width), width)
        pick_refs[d][:, :width] = line_ref[:, quarter]
        pick_refs[d][:, width:] = terms


def pick_slots(gebhart, change, moved_nodes):
    nodes, count = change.shape
    chunks = 4
    vmem = pl.BlockSpec(memory_space=pltpu.VMEM)
    hbm = pl.BlockSpec(memory_space=pl.ANY)
    *picked, table = pl.pallas_call(
        pick_kernel,
        out_shape=(jax.ShapeDtypeStruct((SLOTS, nodes // XS + count), jnp.float32),) * XS
        + (jax.ShapeDtypeStruct((8, count), jnp.int32),),
        in_specs=[vmem, hbm, hbm],
        out_specs=(vmem,) * (XS + 1),
        scratch_shapes=[
            pltpu.VMEM((SLOTS, nodes), jnp.float32),
            pltpu.VMEM((nodes, count), jnp.float32),
            pltpu.VMEM((nodes, 2 * count), jnp.bfloat16),
            pltpu.SemaphoreType.DMA((SLOTS,)),
            pltpu.SemaphoreType.DMA((chunks,)),
        ],
        compiler_params=pltpu.CompilerParams(vmem_limit_bytes=60 * 1024 * 1024),
        name="pick_slots",
    )(moved_nodes.reshape(1, count), gebhart, change)
    return picked, table


def respond_kernel(token_ref, g_ref, change_ref, out_ref, kept_ref, lines_ref, g_sem, c_sem):
    rows, count = out_ref.shape
    chunks = g_sem.shape[0]
    block = kept_ref.shape[1] // chunks
    copies = []
    for i in range(chunks):
        span = pl.ds(i * block, block)
        copies.append((
            pltpu.make_async_copy(g_ref.at[:, span], kept_ref.at[:, span], g_sem.at[i]),
            pltpu.make_async_copy(change_ref.at[span, :], lines_ref.at[span, :], c_sem.at[i]),
        ))
        for copy in copies[-1]:
            copy.start()
    total = jnp.zeros((rows, count), jnp.float32)
    for i in range(chunks):
        for copy in copies[i]:
            copy.wait()
        g_high, g_low = split(kept_ref[:, i * block:(i + 1) * block])
        c_high, c_low = split(lines_ref[i * block:(i + 1) * block, :])
        wide_sum = jnp.dot(g_high, jnp.concatenate([c_high, c_low], axis=1), preferred_element_type=jnp.float32)
        low_sum = jnp.dot(g_low, c_high, preferred_element_type=jnp.float32)
        total = total + (wide_sum[:, :count] + (wide_sum[:, count:] + low_sum))
    out_ref[...] = total


def respond(token, gebhart, change):
    rows, nodes = gebhart.shape
    count = change.shape[1]
    chunks = 8
    vmem = pl.BlockSpec(memory_space=pltpu.VMEM)
    hbm = pl.BlockSpec(memory_space=pl.ANY)
    return pl.pallas_call(
        respond_kernel,
        out_shape=jax.ShapeDtypeStruct((rows, count), jnp.float32),
        in_specs=[vmem, hbm, hbm],
        out_specs=vmem,
        scratch_shapes=[
            pltpu.VMEM((rows, nodes), jnp.float32),
            pltpu.VMEM((nodes, count), jnp.float32),
            pltpu.SemaphoreType.DMA((chunks,)),
            pltpu.SemaphoreType.DMA((chunks,)),
        ],
        cost_estimate=pl.CostEstimate(flops=800_000_000, bytes_accessed=8_000_000, transcendentals=0),
        compiler_params=pltpu.CompilerParams(vmem_limit_bytes=24 * 1024 * 1024),
        name="respond",
    )(token, gebhart, change)


def plane_kernel(table_ref, *refs):
    slots_refs, out_ref, rows_ref = refs[:-2], refs[-2], refs[-1]
    copies, plane, columns = out_ref.shape
    count = table_ref.shape[1]
    core = lax.axis_index("wide") % CORES
    part = columns - count
    width = CORES * part
    for i, ref in enumerate(slots_refs):
        value = ref[...]
        here = slice(i * SLOTS, (i + 1) * SLOTS)
        rows_ref[here, :part] = jnp.where(core == 0, value[:, :part], value[:, part:width])
        rows_ref[here, part:] = value[:, width:]
    for i in range(plane):
        out_ref[0, i:i + 1, :] = rows_ref[pl.ds(table_ref[1, i], 1), :]
    value = out_ref[0]
    for copy in range(1, copies):
        out_ref[copy] = value


def plane_slots(table, slots, planes, room):
    count = table.shape[1]
    columns = (slots[0].shape[1] - count) // CORES + count
    vmem = pl.BlockSpec(memory_space=pltpu.VMEM)
    return pl.pallas_call(
        plane_kernel,
        out_shape=jax.ShapeDtypeStruct((planes, room, columns), jnp.float32),
        in_specs=[pl.BlockSpec(memory_space=pltpu.SMEM)] + [vmem] * len(slots),
        out_specs=vmem,
        scratch_shapes=[pltpu.VMEM((len(slots) * SLOTS, columns), jnp.float32)],
        compiler_params=pltpu.CompilerParams(vmem_limit_bytes=16 * 1024 * 1024),
        name="plane_slots",
    )(table, *slots)


def order_kernel(table_ref, slots_ref, rows_ref, touched_ref):
    count, part = rows_ref.shape

    def move(k, carry):
        row = slots_ref[pl.ds(table_ref[0, k], 1), :]
        rows_ref[pl.ds(k, 1), :] = row[:, :part]
        touched_ref[pl.ds(k, 1), :] = row[:, part:]
        return carry

    lax.fori_loop(0, count, move, 0, unroll=8)


def order(table, slots):
    count = table.shape[1]
    part = slots.shape[1] - count
    vmem = pl.BlockSpec(memory_space=pltpu.VMEM)
    return pl.pallas_call(
        order_kernel,
        out_shape=(jax.ShapeDtypeStruct((count, part), jnp.float32), jax.ShapeDtypeStruct((count, count), jnp.float32)),
        in_specs=[pl.BlockSpec(memory_space=pltpu.SMEM), vmem],
        out_specs=(vmem, vmem),
        compiler_params=pltpu.CompilerParams(vmem_limit_bytes=16 * 1024 * 1024),
        name="order_rows",
    )(table, slots)


def pick_all_kernel(moved_ref, g_ref, keep_ref, send_ref, sem):
    rows_local = g_ref.shape[0]
    quarters, half, width = keep_ref.shape
    me = lax.axis_index("wide")
    first = me * rows_local
    core = me % CORES

    def copy(local, target, row, q):
        return pltpu.make_async_copy(
            g_ref.at[pl.ds(local, 1), pl.ds(q * width, width)], target.at[q, pl.ds(row, 1), :], sem
        )

    total = 0
    for side in range(CORES):
        def start(row, found, side=side):
            local = moved_ref[side * half + row] - first
            owned = jnp.logical_and(local >= 0, local < rows_local)

            @pl.when(owned)
            def _():
                @pl.when(core == side)
                def _():
                    for q in range(quarters):
                        copy(local, keep_ref, row, q).start()

                @pl.when(core != side)
                def _():
                    for q in range(quarters):
                        copy(local, send_ref, row, q).start()

            return found + jnp.where(owned, 1, 0)

        total = lax.fori_loop(0, half, start, total, unroll=8)

    def wait(i, carry):
        for q in range(quarters):
            copy(0, keep_ref, 0, q).wait()
        return carry

    lax.fori_loop(0, total, wait, 0)


def pick_all(gebhart, moved_nodes, half, width):
    shape = jax.ShapeDtypeStruct((XS, half, width), jnp.float32)
    return pl.pallas_call(
        pick_all_kernel,
        out_shape=(shape, shape),
        in_specs=[pl.BlockSpec(memory_space=pltpu.SMEM), pl.BlockSpec(memory_space=pl.ANY)],
        out_specs=(pl.BlockSpec(memory_space=pl.ANY), pl.BlockSpec(memory_space=pl.ANY)),
        scratch_shapes=[pltpu.SemaphoreType.DMA],
        compiler_params=pltpu.CompilerParams(vmem_limit_bytes=60 * 1024 * 1024),
        name="pick_rows",
    )(moved_nodes, gebhart)


def split(value):
    high = value.astype(jnp.bfloat16)
    low = (value - high.astype(jnp.float32)).astype(jnp.bfloat16)
    return high, low


def pair_inverse(p, q, s):
    scale = 1.0 / (p * s - q * q)
    return s * scale, -q * scale, p * scale


def quad_inverse(e):
    a, b, c = pair_inverse(e[0][0], e[0][1], e[1][1])
    t = [[a * e[0][2] + b * e[1][2], a * e[0][3] + b * e[1][3]], [b * e[0][2] + c * e[1][2], b * e[0][3] + c * e[1][3]]]
    s22 = e[2][2] - (e[0][2] * t[0][0] + e[1][2] * t[1][0])
    s23 = e[2][3] - (e[0][2] * t[0][1] + e[1][2] * t[1][1])
    s33 = e[3][3] - (e[0][3] * t[0][1] + e[1][3] * t[1][1])
    f, g, h = pair_inverse(s22, s23, s33)
    w = [[t[0][0] * f + t[0][1] * g, t[0][0] * g + t[0][1] * h], [t[1][0] * f + t[1][1] * g, t[1][0] * g + t[1][1] * h]]
    i00 = a + w[0][0] * t[0][0] + w[0][1] * t[0][1]
    i01 = b + w[0][0] * t[1][0] + w[0][1] * t[1][1]
    i11 = c + w[1][0] * t[1][0] + w[1][1] * t[1][1]
    return [
        [i00, i01, -w[0][0], -w[0][1]],
        [i01, i11, -w[1][0], -w[1][1]],
        [-w[0][0], -w[1][0], f, g],
        [-w[0][1], -w[1][1], g, h],
    ]


def spd_inverse(normal, block=16):
    pivots = 4
    count = normal.shape[0]
    lane = lax.broadcasted_iota(jnp.int32, (1, count), 1)
    sub = lax.broadcasted_iota(jnp.int32, (block, 1), 0)
    for first in range(0, count, block):
        panel = normal[first:first + block, :]
        for i in range(0, block, pivots):
            k = first + i
            cols = [jnp.broadcast_to(panel[:, k + m:k + m + 1], (block, count)) for m in range(pivots)]
            entry = [[jnp.broadcast_to(cols[n][i + m:i + m + 1, :], (8, count)) for n in range(pivots)] for m in range(pivots)]
            q = quad_inverse(entry)
            inside = jnp.logical_and(lane >= k, lane < k + pivots)
            rows = [
                jnp.where(inside, jnp.where(lane == k + m, 1.0, 0.0), jnp.broadcast_to(panel[i + m:i + m + 1, :], (8, count)))
                for m in range(pivots)
            ]
            new = [q[m][0] * rows[0] + (q[m][1] * rows[1] + (q[m][2] * rows[2] + q[m][3] * rows[3])) for m in range(pivots)]
            new = [jnp.concatenate([row] * (block // 8), axis=0) for row in new]
            panel = jnp.where(inside, 0.0, panel)
            for m in range(pivots):
                panel = panel - cols[m] * new[m]
            for m in range(pivots):
                panel = jnp.where(sub == i + m, new[m], panel)
        within = jnp.logical_and(lane >= first, lane < first + block)
        outer = jnp.dot(normal[:, first:first + block], panel, precision=HIGHEST, preferred_element_type=jnp.float32)
        rest = jnp.where(within, 0.0, normal) - outer
        above = [rest[:first]] if first > 0 else []
        below = [rest[first + block:]] if first + block < count else []
        normal = jnp.concatenate(above + [panel] + below, axis=0)
    return normal


def invert_kernel(*refs):
    out_ref = refs[-1]
    touched = refs[0][...]
    for ref in refs[1:-1]:
        touched = touched + ref[...]
    count = touched.shape[0]
    row = lax.broadcasted_iota(jnp.int32, (count, count), 0)
    column = lax.broadcasted_iota(jnp.int32, (count, count), 1)
    capacitance = jnp.where(row == column, 1.0, 0.0) - touched
    normal = lax.dot_general(
        capacitance, capacitance, (((1,), (1,)), ((), ())), precision=HIGHEST, preferred_element_type=jnp.float32
    )
    out_ref[...] = jnp.dot(spd_inverse(normal), capacitance, precision=HIGHEST, preferred_element_type=jnp.float32)


def invert(parts):
    vmem = pl.BlockSpec(memory_space=pltpu.VMEM)
    return pl.pallas_call(
        invert_kernel,
        out_shape=jax.ShapeDtypeStruct(parts[0].shape, jnp.float32),
        in_specs=[vmem] * len(parts),
        out_specs=vmem,
        cost_estimate=pl.CostEstimate(flops=2_000_000_000, bytes_accessed=8_000_000, transcendentals=0),
        compiler_params=pltpu.CompilerParams(vmem_limit_bytes=16 * 1024 * 1024),
        name="invert_capacitance",
    )(*parts)


def places(core, part):
    x = (lax.axis_index("wide") // CORES) % XS
    return [pl.ds(pl.multiple_of((lax.rem(x + (XS - d), XS) * CORES + core) * part, part), part) for d in range(XS)]


def write_blocks(left, g_ref, pieces, out_ref, buffer_ref, sem, core):
    copies = []
    for d, here in enumerate(places(core, pieces[0].shape[1])):
        r_high, r_low = split(pieces[d][...])
        right = jnp.concatenate([r_high, r_high, r_low], axis=0)
        buffer_ref[d] = g_ref[:, here] + jnp.dot(left, right, preferred_element_type=jnp.float32)
        copies.append(pltpu.make_async_copy(buffer_ref.at[d], out_ref.at[:, here], sem.at[d]))
        copies[d].start()
    for copy in copies:
        copy.wait()


def update_own_kernel(inverse_ref, g_ref, *refs):
    pieces, response_refs, (out_ref, left_ref, buffer_ref, sem) = refs[:XS], refs[XS:-4], refs[-4:]
    response = response_refs[0][...]
    for ref in response_refs[1:]:
        response = response + ref[...]
    solved = lax.dot_general(
        response, inverse_ref[...], (((1,), (1,)), ((), ())), precision=HIGHEST, preferred_element_type=jnp.float32
    )
    s_high, s_low = split(solved)
    left = jnp.concatenate([s_high, s_low, s_high], axis=1)
    left_ref[...] = left
    write_blocks(left, g_ref, pieces, out_ref, buffer_ref, sem, lax.axis_index("wide") % CORES)


def update_other_kernel(left_ref, g_ref, before_ref, *refs):
    pieces, (out_ref, buffer_ref, sem) = refs[:XS], refs[XS:]
    write_blocks(left_ref[...], g_ref, pieces, out_ref, buffer_ref, sem, 1 - lax.axis_index("wide") % CORES)


def update(gebhart, inverse, response, pieces, swapped):
    rows, nodes = gebhart.shape
    count, part = pieces[0].shape
    vmem = pl.BlockSpec(memory_space=pltpu.VMEM)
    hbm = pl.BlockSpec(memory_space=pl.ANY)
    whole = jax.ShapeDtypeStruct((rows, nodes), jnp.float32)
    scratch = [pltpu.VMEM((XS, rows, part), jnp.float32), pltpu.SemaphoreType.DMA((XS,))]
    params = pltpu.CompilerParams(vmem_limit_bytes=16 * 1024 * 1024)
    own, left = pl.pallas_call(
        update_own_kernel,
        out_shape=(whole, jax.ShapeDtypeStruct((rows, 3 * count), jnp.bfloat16)),
        in_specs=[vmem] * (2 + XS + len(response)),
        out_specs=(hbm, vmem),
        scratch_shapes=scratch,
        cost_estimate=pl.CostEstimate(flops=1_000_000_000, bytes_accessed=6_000_000, transcendentals=0),
        compiler_params=params,
        name="update_own",
    )(inverse, gebhart, *pieces, *response)
    return pl.pallas_call(
        update_other_kernel,
        out_shape=whole,
        in_specs=[vmem, vmem, hbm] + [vmem] * XS,
        out_specs=hbm,
        scratch_shapes=scratch,
        input_output_aliases={2: 0},
        compiler_params=params,
        name="update_other",
    )(left, gebhart, own, *swapped)


def body(wide, narrow, gebhart, change, moved_nodes):
    rows_local, width_local = gebhart.shape
    count = moved_nodes.shape[0]
    half = count // CORES
    zs = wide // (CORES * XS)
    width = width_local // XS
    group = half // zs
    me = lax.axis_index("wide")
    core = me % CORES
    x = (me // CORES) % XS
    z = me // (CORES * XS)

    def index(z, x, c):
        return (z * XS + x) * CORES + c

    places = [(z, x, c) for z in range(zs) for x in range(XS) for c in range(CORES)]
    swap = [(index(z, x, c), index(z, x, (c + 1) % CORES)) for z, x, c in places]
    shift_x = [[(index(z, x, c), index(z, (x + d) % XS, c)) for z, x, c in places] for d in range(XS)]
    shift_y = [[(i, (i + d) % narrow) for i in range(narrow)] for d in range(narrow)]
    x_groups = [[index(z, x, c) for x in range(XS)] for z in range(zs) for c in range(CORES)]
    z_groups = [[index(z, x, c) for z in range(zs)] for x in range(XS) for c in range(CORES)]

    part = width // CORES
    picked, table = pick_slots(gebhart, change, moved_nodes)

    def received(value):
        return [lax.ppermute(value, "narrow", shift_y[d]) for d in range(1, narrow)]

    own = [picked[0]] + [lax.ppermute(picked[d], "wide", shift_x[d]) for d in range(1, XS)]
    other = [lax.ppermute(slots, "wide", swap) for slots in own]

    def spread(room, gebhart, change, moved_nodes, slots, table):
        slots = plane_slots(table, slots, zs, room)
        slots, token = lax.optimization_barrier((slots, table))
        partial_value = respond(token, gebhart, change)
        response = [partial_value] + received(partial_value)
        slots = lax.all_to_all(slots, "wide", 0, 0, axis_index_groups=z_groups)
        slots, response = lax.optimization_barrier((slots, response))
        return tuple(order(table, slots.reshape(zs * room, part + count))) + tuple(response)

    def crowded(gebhart, change, moved_nodes, slots, table):
        partial_value = respond(table, gebhart, change)
        owner = moved_nodes // rows_local
        owner_half = lax.dynamic_slice(owner, (core * half,), (half,))
        owner_core = owner_half % CORES
        owner_x = (owner_half // CORES) % XS
        owner_z = lax.dynamic_slice(owner_half // (CORES * XS), (z * group,), (group,))

        keep, send = pick_all(gebhart, moved_nodes, half, width)
        got = lax.ppermute(send, "wide", swap)
        positions = me * rows_local + lax.broadcasted_iota(jnp.int32, (count, rows_local), 1)
        select = (moved_nodes[:, None] == positions).astype(jnp.float32)
        terms = jnp.dot(select, partial_value, preferred_element_type=jnp.float32, precision=HIGHEST)
        terms_mine = lax.dynamic_slice(terms, (core * half, 0), (half, count))
        terms_theirs = lax.dynamic_slice(terms, ((1 - core) * half, 0), (half, count))
        terms_chip = terms_mine + lax.ppermute(terms_theirs, "wide", swap)

        rows_chip = jnp.where((owner_core == core)[None, :, None], keep, got)
        both = jnp.concatenate([rows_chip, jnp.broadcast_to(terms_chip[None], (XS, half, count))], axis=2)
        both = lax.all_to_all(both, "wide", 0, 0, axis_index_groups=x_groups)
        chosen = owner_x[None, :, None] == lax.broadcasted_iota(jnp.int32, (XS, 1, 1), 0)
        both = jnp.sum(jnp.where(chosen, both, 0.0), axis=0)

        both = lax.all_to_all(both.reshape(zs, group, width + count), "wide", 0, 0, axis_index_groups=z_groups)
        chosen = owner_z[None, :, None] == lax.broadcasted_iota(jnp.int32, (zs, 1, 1), 0)
        both = jnp.sum(jnp.where(chosen, both, 0.0), axis=0)
        both = lax.all_to_all(jnp.broadcast_to(both[None], (zs,) + both.shape), "wide", 0, 0, axis_index_groups=z_groups)
        both = both.reshape(half, width + count)

        mine = jnp.concatenate([lax.dynamic_slice(both, (0, core * part), (half, part)), both[:, width:]], axis=1)
        theirs = jnp.concatenate([lax.dynamic_slice(both, (0, (1 - core) * part), (half, part)), both[:, width:]], axis=1)
        theirs = lax.ppermute(theirs, "wide", swap)
        both = jnp.where(core == 0, jnp.concatenate([mine, theirs]), jnp.concatenate([theirs, mine]))
        return (both[:, :part], both[:, part:], partial_value) + tuple(received(partial_value))

    paths = [functools.partial(spread, room) for room in PLANES] + [crowded]
    rows, touched, *response = lax.switch(table[2, 0], paths, gebhart, change, moved_nodes, own + other, table)

    pieces = [rows] + [lax.ppermute(rows, "wide", shift_x[d]) for d in range(1, XS)]
    inverse = invert([touched] + received(touched))
    pieces, inverse = lax.optimization_barrier((pieces, inverse))
    return update(gebhart, inverse, response, pieces, [lax.ppermute(piece, "wide", swap) for piece in pieces])


def solution(mesh):
    return jax.shard_map(
        functools.partial(body, mesh.shape["wide"], mesh.shape["narrow"]),
        mesh=mesh,
        in_specs=(P("wide", "narrow"), P("narrow", None), P()),
        out_specs=P("wide", "narrow"),
        check_vma=False,
    )
```

```python
import functools

import jax
import jax.numpy as jnp
from jax import lax
from jax.experimental import pallas as pl
from jax.experimental.pallas import tpu as pltpu
from jax.sharding import PartitionSpec as P

HIGHEST = lax.Precision.HIGHEST
CORES = 2
XS = 4
SLOTS = 16
PLANES = (24, 32)


def pick_kernel(lanes_ref, g_ref, change_ref, *refs):
    pick_refs, table_ref, line_ref, lines_ref, halves_ref, row_sem, sem = refs[:XS], *refs[XS:]
    nodes, count = lines_ref.shape
    rows = g_ref.shape[0]
    width = nodes // XS
    chunks = sem.shape[0]
    block = nodes // chunks
    me = lax.axis_index("wide")
    first = me * rows
    x = (me // CORES) % XS

    copies = []
    for i in range(chunks):
        span = pl.ds(i * block, block)
        copies.append(pltpu.make_async_copy(change_ref.at[span, :], lines_ref.at[span, :], sem.at[i]))
        copies[i].start()

    node_across = jnp.broadcast_to(lanes_ref[...].astype(jnp.float32), (count, count))
    node_down = node_across.T
    across = jnp.floor(node_across / float(rows))
    down = jnp.floor(node_down / float(rows))
    i = lax.broadcasted_iota(jnp.int32, (count, count), 0)
    j = lax.broadcasted_iota(jnp.int32, (count, count), 1)
    one = jnp.where(across == down, 1.0, 0.0)
    slot = jnp.sum(jnp.where(j < i, one, 0.0), axis=1, keepdims=True)
    match = jnp.logical_and(down == me.astype(jnp.float32), slot == j.astype(jnp.float32))
    local = jnp.sum(jnp.where(match, node_down - first.astype(jnp.float32), 0.0), axis=0, keepdims=True).astype(jnp.int32)
    picks = []
    for s in range(SLOTS):
        picks.append(pltpu.make_async_copy(g_ref.at[pl.ds(local[0, s], 1), :], line_ref.at[pl.ds(s, 1), :], row_sem.at[s]))
        picks[s].start()

    per_plane = float(CORES * XS)
    plane_across = jnp.floor(across / per_plane)
    plane_down = jnp.floor(down / per_plane)
    plane = jnp.where(plane_across == plane_down, 1.0, 0.0)
    rank = jnp.sum(jnp.where(j < i, plane, 0.0), axis=1, keepdims=True)
    rank_across = jnp.sum(jnp.where(i < j, plane, 0.0), axis=0, keepdims=True)
    most = jnp.max(rank)
    path = len(PLANES)
    room = float(PLANES[-1])
    for choice in reversed(range(len(PLANES))):
        path = jnp.where(most < PLANES[choice], choice, path)
        room = jnp.where(most < PLANES[choice], float(PLANES[choice]), room)
    path = jnp.where(jnp.max(slot) < SLOTS, path, len(PLANES))
    inside = down - plane_down * per_plane
    x_down = jnp.floor(inside / float(CORES))
    core_down = inside - x_down * float(CORES)
    behind = x.astype(jnp.float32) - x_down
    behind = jnp.where(behind < 0, behind + float(XS), behind)
    side = jnp.where(core_down == (me % CORES).astype(jnp.float32), 0.0, float(XS * SLOTS))
    here = plane_down == (me // (CORES * XS)).astype(jnp.float32)
    match = jnp.logical_and(here, rank == j.astype(jnp.float32))
    source = jnp.sum(jnp.where(match, behind * float(SLOTS) + jnp.minimum(slot, SLOTS - 1.0) + side, 0.0), axis=0, keepdims=True)
    target = plane_across[:1] * room + jnp.minimum(rank_across, room - 1.0)
    table_ref[0:1, :] = target.astype(jnp.int32)
    table_ref[1:2, :] = source.astype(jnp.int32)
    table_ref[2:8, :] = jnp.full((6, count), path, jnp.int32)

    for i in range(chunks):
        span = pl.ds(i * block, block)
        copies[i].wait()
        c_high, c_low = split(lines_ref[span, :])
        halves_ref[span, :count] = c_high
        halves_ref[span, count:] = c_low
    for pick in picks:
        pick.wait()
    r_high, r_low = split(line_ref[...])
    both = jnp.dot(jnp.concatenate([r_high, r_low], axis=0), halves_ref[...], preferred_element_type=jnp.float32)
    terms = both[:SLOTS, :count] + (both[:SLOTS, count:] + both[SLOTS:, :count])
    for d in range(XS):
        quarter = pl.ds(pl.multiple_of(lax.rem(x + d, XS) * width, width), width)
        pick_refs[d][:, :width] = line_ref[:, quarter]
        pick_refs[d][:, width:] = terms


def pick_slots(gebhart, change, moved_nodes):
    nodes, count = change.shape
    chunks = 4
    vmem = pl.BlockSpec(memory_space=pltpu.VMEM)
    hbm = pl.BlockSpec(memory_space=pl.ANY)
    *picked, table = pl.pallas_call(
        pick_kernel,
        out_shape=(jax.ShapeDtypeStruct((SLOTS, nodes // XS + count), jnp.float32),) * XS
        + (jax.ShapeDtypeStruct((8, count), jnp.int32),),
        in_specs=[vmem, hbm, hbm],
        out_specs=(vmem,) * (XS + 1),
        scratch_shapes=[
            pltpu.VMEM((SLOTS, nodes), jnp.float32),
            pltpu.VMEM((nodes, count), jnp.float32),
            pltpu.VMEM((nodes, 2 * count), jnp.bfloat16),
            pltpu.SemaphoreType.DMA((SLOTS,)),
            pltpu.SemaphoreType.DMA((chunks,)),
        ],
        compiler_params=pltpu.CompilerParams(vmem_limit_bytes=60 * 1024 * 1024),
        name="pick_slots",
    )(moved_nodes.reshape(1, count), gebhart, change)
    return picked, table


def respond_kernel(token_ref, g_ref, change_ref, out_ref, kept_ref, lines_ref, g_sem, c_sem):
    rows, count = out_ref.shape
    chunks = g_sem.shape[0]
    block = kept_ref.shape[1] // chunks
    copies = []
    for i in range(chunks):
        span = pl.ds(i * block, block)
        copies.append((
            pltpu.make_async_copy(g_ref.at[:, span], kept_ref.at[:, span], g_sem.at[i]),
            pltpu.make_async_copy(change_ref.at[span, :], lines_ref.at[span, :], c_sem.at[i]),
        ))
        for copy in copies[-1]:
            copy.start()
    total = jnp.zeros((rows, count), jnp.float32)
    for i in range(chunks):
        for copy in copies[i]:
            copy.wait()
        g_high, g_low = split(kept_ref[:, i * block:(i + 1) * block])
        c_high, c_low = split(lines_ref[i * block:(i + 1) * block, :])
        wide_sum = jnp.dot(g_high, jnp.concatenate([c_high, c_low], axis=1), preferred_element_type=jnp.float32)
        low_sum = jnp.dot(g_low, c_high, preferred_element_type=jnp.float32)
        total = total + (wide_sum[:, :count] + (wide_sum[:, count:] + low_sum))
    out_ref[...] = total


def respond(token, gebhart, change):
    rows, nodes = gebhart.shape
    count = change.shape[1]
    chunks = 8
    vmem = pl.BlockSpec(memory_space=pltpu.VMEM)
    hbm = pl.BlockSpec(memory_space=pl.ANY)
    return pl.pallas_call(
        respond_kernel,
        out_shape=jax.ShapeDtypeStruct((rows, count), jnp.float32),
        in_specs=[vmem, hbm, hbm],
        out_specs=vmem,
        scratch_shapes=[
            pltpu.VMEM((rows, nodes), jnp.float32),
            pltpu.VMEM((nodes, count), jnp.float32),
            pltpu.SemaphoreType.DMA((chunks,)),
            pltpu.SemaphoreType.DMA((chunks,)),
        ],
        cost_estimate=pl.CostEstimate(flops=800_000_000, bytes_accessed=8_000_000, transcendentals=0),
        compiler_params=pltpu.CompilerParams(vmem_limit_bytes=24 * 1024 * 1024),
        name="respond",
    )(token, gebhart, change)


def plane_kernel(table_ref, *refs):
    slots_refs, out_ref, rows_ref = refs[:-2], refs[-2], refs[-1]
    copies, plane, columns = out_ref.shape
    count = table_ref.shape[1]
    core = lax.axis_index("wide") % CORES
    part = columns - count
    width = CORES * part
    for i, ref in enumerate(slots_refs):
        value = ref[...]
        here = slice(i * SLOTS, (i + 1) * SLOTS)
        rows_ref[here, :part] = jnp.where(core == 0, value[:, :part], value[:, part:width])
        rows_ref[here, part:] = value[:, width:]
    for i in range(plane):
        out_ref[0, i:i + 1, :] = rows_ref[pl.ds(table_ref[1, i], 1), :]
    value = out_ref[0]
    for copy in range(1, copies):
        out_ref[copy] = value


def plane_slots(table, slots, planes, room):
    count = table.shape[1]
    columns = (slots[0].shape[1] - count) // CORES + count
    vmem = pl.BlockSpec(memory_space=pltpu.VMEM)
    return pl.pallas_call(
        plane_kernel,
        out_shape=jax.ShapeDtypeStruct((planes, room, columns), jnp.float32),
        in_specs=[pl.BlockSpec(memory_space=pltpu.SMEM)] + [vmem] * len(slots),
        out_specs=vmem,
        scratch_shapes=[pltpu.VMEM((len(slots) * SLOTS, columns), jnp.float32)],
        compiler_params=pltpu.CompilerParams(vmem_limit_bytes=16 * 1024 * 1024),
        name="plane_slots",
    )(table, *slots)


def order_kernel(table_ref, slots_ref, rows_ref, touched_ref):
    count, part = rows_ref.shape

    def move(k, carry):
        row = slots_ref[pl.ds(table_ref[0, k], 1), :]
        rows_ref[pl.ds(k, 1), :] = row[:, :part]
        touched_ref[pl.ds(k, 1), :] = row[:, part:]
        return carry

    lax.fori_loop(0, count, move, 0, unroll=8)


def order(table, slots):
    count = table.shape[1]
    part = slots.shape[1] - count
    vmem = pl.BlockSpec(memory_space=pltpu.VMEM)
    return pl.pallas_call(
        order_kernel,
        out_shape=(jax.ShapeDtypeStruct((count, part), jnp.float32), jax.ShapeDtypeStruct((count, count), jnp.float32)),
        in_specs=[pl.BlockSpec(memory_space=pltpu.SMEM), vmem],
        out_specs=(vmem, vmem),
        compiler_params=pltpu.CompilerParams(vmem_limit_bytes=16 * 1024 * 1024),
        name="order_rows",
    )(table, slots)


def pick_all_kernel(moved_ref, g_ref, keep_ref, send_ref, sem):
    rows_local = g_ref.shape[0]
    quarters, half, width = keep_ref.shape
    me = lax.axis_index("wide")
    first = me * rows_local
    core = me % CORES

    def copy(local, target, row, q):
        return pltpu.make_async_copy(
            g_ref.at[pl.ds(local, 1), pl.ds(q * width, width)], target.at[q, pl.ds(row, 1), :], sem
        )

    total = 0
    for side in range(CORES):
        def start(row, found, side=side):
            local = moved_ref[side * half + row] - first
            owned = jnp.logical_and(local >= 0, local < rows_local)

            @pl.when(owned)
            def _():
                @pl.when(core == side)
                def _():
                    for q in range(quarters):
                        copy(local, keep_ref, row, q).start()

                @pl.when(core != side)
                def _():
                    for q in range(quarters):
                        copy(local, send_ref, row, q).start()

            return found + jnp.where(owned, 1, 0)

        total = lax.fori_loop(0, half, start, total, unroll=8)

    def wait(i, carry):
        for q in range(quarters):
            copy(0, keep_ref, 0, q).wait()
        return carry

    lax.fori_loop(0, total, wait, 0)


def pick_all(gebhart, moved_nodes, half, width):
    shape = jax.ShapeDtypeStruct((XS, half, width), jnp.float32)
    return pl.pallas_call(
        pick_all_kernel,
        out_shape=(shape, shape),
        in_specs=[pl.BlockSpec(memory_space=pltpu.SMEM), pl.BlockSpec(memory_space=pl.ANY)],
        out_specs=(pl.BlockSpec(memory_space=pl.ANY), pl.BlockSpec(memory_space=pl.ANY)),
        scratch_shapes=[pltpu.SemaphoreType.DMA],
        compiler_params=pltpu.CompilerParams(vmem_limit_bytes=60 * 1024 * 1024),
        name="pick_rows",
    )(moved_nodes, gebhart)


def split(value):
    high = value.astype(jnp.bfloat16)
    low = (value - high.astype(jnp.float32)).astype(jnp.bfloat16)
    return high, low


def pair_inverse(p, q, s):
    scale = 1.0 / (p * s - q * q)
    return s * scale, -q * scale, p * scale


def quad_inverse(e):
    a, b, c = pair_inverse(e[0][0], e[0][1], e[1][1])
    t = [[a * e[0][2] + b * e[1][2], a * e[0][3] + b * e[1][3]], [b * e[0][2] + c * e[1][2], b * e[0][3] + c * e[1][3]]]
    s22 = e[2][2] - (e[0][2] * t[0][0] + e[1][2] * t[1][0])
    s23 = e[2][3] - (e[0][2] * t[0][1] + e[1][2] * t[1][1])
    s33 = e[3][3] - (e[0][3] * t[0][1] + e[1][3] * t[1][1])
    f, g, h = pair_inverse(s22, s23, s33)
    w = [[t[0][0] * f + t[0][1] * g, t[0][0] * g + t[0][1] * h], [t[1][0] * f + t[1][1] * g, t[1][0] * g + t[1][1] * h]]
    i00 = a + w[0][0] * t[0][0] + w[0][1] * t[0][1]
    i01 = b + w[0][0] * t[1][0] + w[0][1] * t[1][1]
    i11 = c + w[1][0] * t[1][0] + w[1][1] * t[1][1]
    return [
        [i00, i01, -w[0][0], -w[0][1]],
        [i01, i11, -w[1][0], -w[1][1]],
        [-w[0][0], -w[1][0], f, g],
        [-w[0][1], -w[1][1], g, h],
    ]


def spd_inverse(normal, block=16):
    pivots = 4
    count = normal.shape[0]
    lane = lax.broadcasted_iota(jnp.int32, (1, count), 1)
    sub = lax.broadcasted_iota(jnp.int32, (block, 1), 0)
    for first in range(0, count, block):
        panel = normal[first:first + block, :]
        for i in range(0, block, pivots):
            k = first + i
            cols = [jnp.broadcast_to(panel[:, k + m:k + m + 1], (block, count)) for m in range(pivots)]
            entry = [[jnp.broadcast_to(cols[n][i + m:i + m + 1, :], (8, count)) for n in range(pivots)] for m in range(pivots)]
            q = quad_inverse(entry)
            inside = jnp.logical_and(lane >= k, lane < k + pivots)
            rows = [
                jnp.where(inside, jnp.where(lane == k + m, 1.0, 0.0), jnp.broadcast_to(panel[i + m:i + m + 1, :], (8, count)))
                for m in range(pivots)
            ]
            new = [q[m][0] * rows[0] + (q[m][1] * rows[1] + (q[m][2] * rows[2] + q[m][3] * rows[3])) for m in range(pivots)]
            new = [jnp.concatenate([row] * (block // 8), axis=0) for row in new]
            panel = jnp.where(inside, 0.0, panel)
            for m in range(pivots):
                panel = panel - cols[m] * new[m]
            for m in range(pivots):
                panel = jnp.where(sub == i + m, new[m], panel)
        within = jnp.logical_and(lane >= first, lane < first + block)
        outer = jnp.dot(normal[:, first:first + block], panel, precision=HIGHEST, preferred_element_type=jnp.float32)
        rest = jnp.where(within, 0.0, normal) - outer
        above = [rest[:first]] if first > 0 else []
        below = [rest[first + block:]] if first + block < count else []
        normal = jnp.concatenate(above + [panel] + below, axis=0)
    return normal


def solve_kernel(narrow, *refs):
    left_ref, buffer_ref, sem = refs[-3:]
    touched_refs, response_refs = refs[:-3 - narrow], refs[-3 - narrow:-3]
    copies = []
    for i, ref in enumerate(response_refs):
        copies.append(pltpu.make_async_copy(ref, buffer_ref.at[i], sem.at[i]))
        copies[i].start()
    touched = touched_refs[0][...]
    for ref in touched_refs[1:]:
        touched = touched + ref[...]
    count = touched.shape[0]
    row = lax.broadcasted_iota(jnp.int32, (count, count), 0)
    column = lax.broadcasted_iota(jnp.int32, (count, count), 1)
    capacitance = jnp.where(row == column, 1.0, 0.0) - touched
    normal = lax.dot_general(
        capacitance, capacitance, (((1,), (1,)), ((), ())), precision=HIGHEST, preferred_element_type=jnp.float32
    )
    inverse = jnp.dot(spd_inverse(normal), capacitance, precision=HIGHEST, preferred_element_type=jnp.float32)
    for copy in copies:
        copy.wait()
    response = buffer_ref[0]
    for i in range(1, narrow):
        response = response + buffer_ref[i]
    solved = lax.dot_general(
        response, inverse, (((1,), (1,)), ((), ())), precision=HIGHEST, preferred_element_type=jnp.float32
    )
    s_high, s_low = split(solved)
    left_ref[...] = jnp.concatenate([s_high, s_low, s_high], axis=1)


def solve(touched, response):
    rows, count = response[0].shape
    narrow = len(response)
    vmem = pl.BlockSpec(memory_space=pltpu.VMEM)
    return pl.pallas_call(
        functools.partial(solve_kernel, narrow),
        out_shape=jax.ShapeDtypeStruct((rows, 3 * count), jnp.bfloat16),
        in_specs=[vmem] * len(touched) + [pl.BlockSpec(memory_space=pl.ANY)] * narrow,
        out_specs=vmem,
        scratch_shapes=[pltpu.VMEM((narrow, rows, count), jnp.float32), pltpu.SemaphoreType.DMA((narrow,))],
        cost_estimate=pl.CostEstimate(flops=2_000_000_000, bytes_accessed=8_000_000, transcendentals=0),
        compiler_params=pltpu.CompilerParams(vmem_limit_bytes=16 * 1024 * 1024),
        name="solve",
    )(*touched, *response)


def places(core, part):
    x = (lax.axis_index("wide") // CORES) % XS
    return [pl.ds(pl.multiple_of((lax.rem(x + (XS - d), XS) * CORES + core) * part, part), part) for d in range(XS)]


def write_blocks(left, g_ref, pieces, out_ref, buffer_ref, sem, core):
    copies = []
    for d, here in enumerate(places(core, pieces[0].shape[1])):
        r_high, r_low = split(pieces[d][...])
        right = jnp.concatenate([r_high, r_high, r_low], axis=0)
        buffer_ref[d] = g_ref[:, here] + jnp.dot(left, right, preferred_element_type=jnp.float32)
        copies.append(pltpu.make_async_copy(buffer_ref.at[d], out_ref.at[:, here], sem.at[d]))
        copies[d].start()
    for copy in copies:
        copy.wait()


def update_own_kernel(left_ref, g_ref, *refs):
    pieces, (out_ref, buffer_ref, sem) = refs[:XS], refs[XS:]
    write_blocks(left_ref[...], g_ref, pieces, out_ref, buffer_ref, sem, lax.axis_index("wide") % CORES)


def update_other_kernel(left_ref, g_ref, before_ref, *refs):
    pieces, (out_ref, buffer_ref, sem) = refs[:XS], refs[XS:]
    write_blocks(left_ref[...], g_ref, pieces, out_ref, buffer_ref, sem, 1 - lax.axis_index("wide") % CORES)


def update(gebhart, left, pieces, swapped):
    rows, nodes = gebhart.shape
    part = pieces[0].shape[1]
    vmem = pl.BlockSpec(memory_space=pltpu.VMEM)
    hbm = pl.BlockSpec(memory_space=pl.ANY)
    whole = jax.ShapeDtypeStruct((rows, nodes), jnp.float32)
    scratch = [pltpu.VMEM((XS, rows, part), jnp.float32), pltpu.SemaphoreType.DMA((XS,))]
    params = pltpu.CompilerParams(vmem_limit_bytes=16 * 1024 * 1024)
    own = pl.pallas_call(
        update_own_kernel,
        out_shape=whole,
        in_specs=[vmem] * (2 + XS),
        out_specs=hbm,
        scratch_shapes=scratch,
        cost_estimate=pl.CostEstimate(flops=1_000_000_000, bytes_accessed=6_000_000, transcendentals=0),
        compiler_params=params,
        name="update_own",
    )(left, gebhart, *pieces)
    return pl.pallas_call(
        update_other_kernel,
        out_shape=whole,
        in_specs=[vmem, vmem, hbm] + [vmem] * XS,
        out_specs=hbm,
        scratch_shapes=scratch,
        input_output_aliases={2: 0},
        compiler_params=params,
        name="update_other",
    )(left, gebhart, own, *swapped)


def body(wide, narrow, gebhart, change, moved_nodes):
    rows_local, width_local = gebhart.shape
    count = moved_nodes.shape[0]
    half = count // CORES
    zs = wide // (CORES * XS)
    width = width_local // XS
    group = half // zs
    me = lax.axis_index("wide")
    core = me % CORES
    x = (me // CORES) % XS
    z = me // (CORES * XS)

    def index(z, x, c):
        return (z * XS + x) * CORES + c

    places = [(z, x, c) for z in range(zs) for x in range(XS) for c in range(CORES)]
    swap = [(index(z, x, c), index(z, x, (c + 1) % CORES)) for z, x, c in places]
    shift_x = [[(index(z, x, c), index(z, (x + d) % XS, c)) for z, x, c in places] for d in range(XS)]
    shift_y = [[(i, (i + d) % narrow) for i in range(narrow)] for d in range(narrow)]
    x_groups = [[index(z, x, c) for x in range(XS)] for z in range(zs) for c in range(CORES)]
    z_groups = [[index(z, x, c) for z in range(zs)] for x in range(XS) for c in range(CORES)]

    part = width // CORES
    picked, table = pick_slots(gebhart, change, moved_nodes)

    def received(value):
        return [lax.ppermute(value, "narrow", shift_y[d]) for d in range(1, narrow)]

    own = [picked[0]] + [lax.ppermute(picked[d], "wide", shift_x[d]) for d in range(1, XS)]
    other = [lax.ppermute(slots, "wide", swap) for slots in own]

    def spread(room, gebhart, change, moved_nodes, slots, table):
        slots = plane_slots(table, slots, zs, room)
        slots, token = lax.optimization_barrier((slots, table))
        partial_value = respond(token, gebhart, change)
        response = [partial_value] + received(partial_value)
        slots = lax.all_to_all(slots, "wide", 0, 0, axis_index_groups=z_groups)
        slots, response = lax.optimization_barrier((slots, response))
        return tuple(order(table, slots.reshape(zs * room, part + count))) + tuple(response)

    def crowded(gebhart, change, moved_nodes, slots, table):
        partial_value = respond(table, gebhart, change)
        owner = moved_nodes // rows_local
        owner_half = lax.dynamic_slice(owner, (core * half,), (half,))
        owner_core = owner_half % CORES
        owner_x = (owner_half // CORES) % XS
        owner_z = lax.dynamic_slice(owner_half // (CORES * XS), (z * group,), (group,))

        keep, send = pick_all(gebhart, moved_nodes, half, width)
        got = lax.ppermute(send, "wide", swap)
        positions = me * rows_local + lax.broadcasted_iota(jnp.int32, (count, rows_local), 1)
        select = (moved_nodes[:, None] == positions).astype(jnp.float32)
        terms = jnp.dot(select, partial_value, preferred_element_type=jnp.float32, precision=HIGHEST)
        terms_mine = lax.dynamic_slice(terms, (core * half, 0), (half, count))
        terms_theirs = lax.dynamic_slice(terms, ((1 - core) * half, 0), (half, count))
        terms_chip = terms_mine + lax.ppermute(terms_theirs, "wide", swap)

        rows_chip = jnp.where((owner_core == core)[None, :, None], keep, got)
        both = jnp.concatenate([rows_chip, jnp.broadcast_to(terms_chip[None], (XS, half, count))], axis=2)
        both = lax.all_to_all(both, "wide", 0, 0, axis_index_groups=x_groups)
        chosen = owner_x[None, :, None] == lax.broadcasted_iota(jnp.int32, (XS, 1, 1), 0)
        both = jnp.sum(jnp.where(chosen, both, 0.0), axis=0)

        both = lax.all_to_all(both.reshape(zs, group, width + count), "wide", 0, 0, axis_index_groups=z_groups)
        chosen = owner_z[None, :, None] == lax.broadcasted_iota(jnp.int32, (zs, 1, 1), 0)
        both = jnp.sum(jnp.where(chosen, both, 0.0), axis=0)
        both = lax.all_to_all(jnp.broadcast_to(both[None], (zs,) + both.shape), "wide", 0, 0, axis_index_groups=z_groups)
        both = both.reshape(half, width + count)

        mine = jnp.concatenate([lax.dynamic_slice(both, (0, core * part), (half, part)), both[:, width:]], axis=1)
        theirs = jnp.concatenate([lax.dynamic_slice(both, (0, (1 - core) * part), (half, part)), both[:, width:]], axis=1)
        theirs = lax.ppermute(theirs, "wide", swap)
        both = jnp.where(core == 0, jnp.concatenate([mine, theirs]), jnp.concatenate([theirs, mine]))
        return (both[:, :part], both[:, part:], partial_value) + tuple(received(partial_value))

    paths = [functools.partial(spread, room) for room in PLANES] + [crowded]
    rows, touched, *response = lax.switch(table[2, 0], paths, gebhart, change, moved_nodes, own + other, table)

    pieces = [rows] + [lax.ppermute(rows, "wide", shift_x[d]) for d in range(1, XS)]
    step = 1
    while step < narrow:
        parts = [touched, lax.ppermute(touched, "narrow", [(i, i ^ step) for i in range(narrow)])]
        touched = parts[0] + parts[1]
        step *= 2
    left = solve(parts, response)
    pieces, left = lax.optimization_barrier((pieces, left))
    return update(gebhart, left, pieces, [lax.ppermute(piece, "wide", swap) for piece in pieces])


def solution(mesh):
    return jax.shard_map(
        functools.partial(body, mesh.shape["wide"], mesh.shape["narrow"]),
        mesh=mesh,
        in_specs=(P("wide", "narrow"), P("narrow", None), P()),
        out_specs=P("wide", "narrow"),
        check_vma=False,
    )
```

```python
import functools

import jax
import jax.numpy as jnp
from jax import lax
from jax.experimental import pallas as pl
from jax.experimental.pallas import tpu as pltpu
from jax.sharding import PartitionSpec as P

HIGHEST = lax.Precision.HIGHEST
CORES = 2
XS = 4
SLOTS = 16
PLANES = (24, 32)


def pick_kernel(lanes_ref, g_ref, change_ref, *refs):
    pick_refs, table_ref, line_ref, lines_ref, halves_ref, row_sem, sem = refs[:XS], *refs[XS:]
    nodes, count = lines_ref.shape
    rows = g_ref.shape[0]
    width = nodes // XS
    chunks = sem.shape[0]
    block = nodes // chunks
    me = lax.axis_index("wide")
    first = me * rows
    x = (me // CORES) % XS

    copies = []
    for i in range(chunks):
        span = pl.ds(i * block, block)
        copies.append(pltpu.make_async_copy(change_ref.at[span, :], lines_ref.at[span, :], sem.at[i]))
        copies[i].start()

    node_across = jnp.broadcast_to(lanes_ref[...].astype(jnp.float32), (count, count))
    node_down = node_across.T
    across = jnp.floor(node_across / float(rows))
    down = jnp.floor(node_down / float(rows))
    i = lax.broadcasted_iota(jnp.int32, (count, count), 0)
    j = lax.broadcasted_iota(jnp.int32, (count, count), 1)
    one = jnp.where(across == down, 1.0, 0.0)
    slot = jnp.sum(jnp.where(j < i, one, 0.0), axis=1, keepdims=True)
    match = jnp.logical_and(down == me.astype(jnp.float32), slot == j.astype(jnp.float32))
    local = jnp.sum(jnp.where(match, node_down - first.astype(jnp.float32), 0.0), axis=0, keepdims=True).astype(jnp.int32)
    picks = []
    for s in range(SLOTS):
        picks.append(pltpu.make_async_copy(g_ref.at[pl.ds(local[0, s], 1), :], line_ref.at[pl.ds(s, 1), :], row_sem.at[s]))
        picks[s].start()

    per_plane = float(CORES * XS)
    plane_across = jnp.floor(across / per_plane)
    plane_down = jnp.floor(down / per_plane)
    plane = jnp.where(plane_across == plane_down, 1.0, 0.0)
    rank = jnp.sum(jnp.where(j < i, plane, 0.0), axis=1, keepdims=True)
    rank_across = jnp.sum(jnp.where(i < j, plane, 0.0), axis=0, keepdims=True)
    most = jnp.max(rank)
    path = len(PLANES)
    room = float(PLANES[-1])
    for choice in reversed(range(len(PLANES))):
        path = jnp.where(most < PLANES[choice], choice, path)
        room = jnp.where(most < PLANES[choice], float(PLANES[choice]), room)
    path = jnp.where(jnp.max(slot) < SLOTS, path, len(PLANES))
    inside = down - plane_down * per_plane
    x_down = jnp.floor(inside / float(CORES))
    core_down = inside - x_down * float(CORES)
    behind = x.astype(jnp.float32) - x_down
    behind = jnp.where(behind < 0, behind + float(XS), behind)
    side = jnp.where(core_down == (me % CORES).astype(jnp.float32), 0.0, float(XS * SLOTS))
    here = plane_down == (me // (CORES * XS)).astype(jnp.float32)
    match = jnp.logical_and(here, rank == j.astype(jnp.float32))
    source = jnp.sum(jnp.where(match, behind * float(SLOTS) + jnp.minimum(slot, SLOTS - 1.0) + side, 0.0), axis=0, keepdims=True)
    target = plane_across[:1] * room + jnp.minimum(rank_across, room - 1.0)
    table_ref[0:1, :] = target.astype(jnp.int32)
    table_ref[1:2, :] = source.astype(jnp.int32)
    table_ref[2:8, :] = jnp.full((6, count), path, jnp.int32)

    for i in range(chunks):
        span = pl.ds(i * block, block)
        copies[i].wait()
        c_high, c_low = split(lines_ref[span, :])
        halves_ref[span, :count] = c_high
        halves_ref[span, count:] = c_low
    for pick in picks:
        pick.wait()
    r_high, r_low = split(line_ref[...])
    both = jnp.dot(jnp.concatenate([r_high, r_low], axis=0), halves_ref[...], preferred_element_type=jnp.float32)
    terms = both[:SLOTS, :count] + (both[:SLOTS, count:] + both[SLOTS:, :count])
    for d in range(XS):
        quarter = pl.ds(pl.multiple_of(lax.rem(x + d, XS) * width, width), width)
        pick_refs[d][:, :width] = line_ref[:, quarter]
        pick_refs[d][:, width:] = terms


def pick_slots(gebhart, change, moved_nodes):
    nodes, count = change.shape
    chunks = 4
    vmem = pl.BlockSpec(memory_space=pltpu.VMEM)
    hbm = pl.BlockSpec(memory_space=pl.ANY)
    *picked, table = pl.pallas_call(
        pick_kernel,
        out_shape=(jax.ShapeDtypeStruct((SLOTS, nodes // XS + count), jnp.float32),) * XS
        + (jax.ShapeDtypeStruct((8, count), jnp.int32),),
        in_specs=[vmem, hbm, hbm],
        out_specs=(vmem,) * (XS + 1),
        scratch_shapes=[
            pltpu.VMEM((SLOTS, nodes), jnp.float32),
            pltpu.VMEM((nodes, count), jnp.float32),
            pltpu.VMEM((nodes, 2 * count), jnp.bfloat16),
            pltpu.SemaphoreType.DMA((SLOTS,)),
            pltpu.SemaphoreType.DMA((chunks,)),
        ],
        compiler_params=pltpu.CompilerParams(vmem_limit_bytes=60 * 1024 * 1024),
        name="pick_slots",
    )(moved_nodes.reshape(1, count), gebhart, change)
    return picked, table


def respond_kernel(token_ref, g_ref, change_ref, out_ref, kept_ref, lines_ref, g_sem, c_sem):
    rows, count = out_ref.shape
    chunks = g_sem.shape[0]
    block = kept_ref.shape[1] // chunks
    copies = []
    for i in range(chunks):
        span = pl.ds(i * block, block)
        copies.append((
            pltpu.make_async_copy(g_ref.at[:, span], kept_ref.at[:, span], g_sem.at[i]),
            pltpu.make_async_copy(change_ref.at[span, :], lines_ref.at[span, :], c_sem.at[i]),
        ))
        for copy in copies[-1]:
            copy.start()
    total = jnp.zeros((rows, count), jnp.float32)
    for i in range(chunks):
        for copy in copies[i]:
            copy.wait()
        g_high, g_low = split(kept_ref[:, i * block:(i + 1) * block])
        c_high, c_low = split(lines_ref[i * block:(i + 1) * block, :])
        wide_sum = jnp.dot(g_high, jnp.concatenate([c_high, c_low], axis=1), preferred_element_type=jnp.float32)
        low_sum = jnp.dot(g_low, c_high, preferred_element_type=jnp.float32)
        total = total + (wide_sum[:, :count] + (wide_sum[:, count:] + low_sum))
    out_ref[...] = total


def respond(token, gebhart, change):
    rows, nodes = gebhart.shape
    count = change.shape[1]
    chunks = 8
    vmem = pl.BlockSpec(memory_space=pltpu.VMEM)
    hbm = pl.BlockSpec(memory_space=pl.ANY)
    return pl.pallas_call(
        respond_kernel,
        out_shape=jax.ShapeDtypeStruct((rows, count), jnp.float32),
        in_specs=[vmem, hbm, hbm],
        out_specs=vmem,
        scratch_shapes=[
            pltpu.VMEM((rows, nodes), jnp.float32),
            pltpu.VMEM((nodes, count), jnp.float32),
            pltpu.SemaphoreType.DMA((chunks,)),
            pltpu.SemaphoreType.DMA((chunks,)),
        ],
        cost_estimate=pl.CostEstimate(flops=800_000_000, bytes_accessed=8_000_000, transcendentals=0),
        compiler_params=pltpu.CompilerParams(vmem_limit_bytes=60 * 1024 * 1024),
        name="respond",
    )(token, gebhart, change)


def plane_kernel(table_ref, *refs):
    slots_refs, out_ref, rows_ref = refs[:-2], refs[-2], refs[-1]
    copies, plane, columns = out_ref.shape
    count = table_ref.shape[1]
    core = lax.axis_index("wide") % CORES
    part = columns - count
    width = CORES * part
    for i, ref in enumerate(slots_refs):
        value = ref[...]
        here = slice(i * SLOTS, (i + 1) * SLOTS)
        rows_ref[here, :part] = jnp.where(core == 0, value[:, :part], value[:, part:width])
        rows_ref[here, part:] = value[:, width:]
    for i in range(plane):
        out_ref[0, i:i + 1, :] = rows_ref[pl.ds(table_ref[1, i], 1), :]
    value = out_ref[0]
    for copy in range(1, copies):
        out_ref[copy] = value


def plane_slots(table, slots, planes, room):
    count = table.shape[1]
    columns = (slots[0].shape[1] - count) // CORES + count
    vmem = pl.BlockSpec(memory_space=pltpu.VMEM)
    return pl.pallas_call(
        plane_kernel,
        out_shape=jax.ShapeDtypeStruct((planes, room, columns), jnp.float32),
        in_specs=[pl.BlockSpec(memory_space=pltpu.SMEM)] + [vmem] * len(slots),
        out_specs=vmem,
        scratch_shapes=[pltpu.VMEM((len(slots) * SLOTS, columns), jnp.float32)],
        compiler_params=pltpu.CompilerParams(vmem_limit_bytes=16 * 1024 * 1024),
        name="plane_slots",
    )(table, *slots)


def order_kernel(table_ref, slots_ref, rows_ref, touched_ref):
    count, part = rows_ref.shape

    def move(k, carry):
        row = slots_ref[pl.ds(table_ref[0, k], 1), :]
        rows_ref[pl.ds(k, 1), :] = row[:, :part]
        touched_ref[pl.ds(k, 1), :] = row[:, part:]
        return carry

    lax.fori_loop(0, count, move, 0, unroll=8)


def order(table, slots):
    count = table.shape[1]
    part = slots.shape[1] - count
    vmem = pl.BlockSpec(memory_space=pltpu.VMEM)
    return pl.pallas_call(
        order_kernel,
        out_shape=(jax.ShapeDtypeStruct((count, part), jnp.float32), jax.ShapeDtypeStruct((count, count), jnp.float32)),
        in_specs=[pl.BlockSpec(memory_space=pltpu.SMEM), vmem],
        out_specs=(vmem, vmem),
        compiler_params=pltpu.CompilerParams(vmem_limit_bytes=16 * 1024 * 1024),
        name="order_rows",
    )(table, slots)


def pick_all_kernel(moved_ref, g_ref, keep_ref, send_ref, sem):
    rows_local = g_ref.shape[0]
    quarters, half, width = keep_ref.shape
    me = lax.axis_index("wide")
    first = me * rows_local
    core = me % CORES

    def copy(local, target, row, q):
        return pltpu.make_async_copy(
            g_ref.at[pl.ds(local, 1), pl.ds(q * width, width)], target.at[q, pl.ds(row, 1), :], sem
        )

    total = 0
    for side in range(CORES):
        def start(row, found, side=side):
            local = moved_ref[side * half + row] - first
            owned = jnp.logical_and(local >= 0, local < rows_local)

            @pl.when(owned)
            def _():
                @pl.when(core == side)
                def _():
                    for q in range(quarters):
                        copy(local, keep_ref, row, q).start()

                @pl.when(core != side)
                def _():
                    for q in range(quarters):
                        copy(local, send_ref, row, q).start()

            return found + jnp.where(owned, 1, 0)

        total = lax.fori_loop(0, half, start, total, unroll=8)

    def wait(i, carry):
        for q in range(quarters):
            copy(0, keep_ref, 0, q).wait()
        return carry

    lax.fori_loop(0, total, wait, 0)


def pick_all(gebhart, moved_nodes, half, width):
    shape = jax.ShapeDtypeStruct((XS, half, width), jnp.float32)
    return pl.pallas_call(
        pick_all_kernel,
        out_shape=(shape, shape),
        in_specs=[pl.BlockSpec(memory_space=pltpu.SMEM), pl.BlockSpec(memory_space=pl.ANY)],
        out_specs=(pl.BlockSpec(memory_space=pl.ANY), pl.BlockSpec(memory_space=pl.ANY)),
        scratch_shapes=[pltpu.SemaphoreType.DMA],
        compiler_params=pltpu.CompilerParams(vmem_limit_bytes=60 * 1024 * 1024),
        name="pick_rows",
    )(moved_nodes, gebhart)


def split(value):
    high = value.astype(jnp.bfloat16)
    low = (value - high.astype(jnp.float32)).astype(jnp.bfloat16)
    return high, low


def pair_inverse(p, q, s):
    scale = 1.0 / (p * s - q * q)
    return s * scale, -q * scale, p * scale


def quad_inverse(e):
    a, b, c = pair_inverse(e[0][0], e[0][1], e[1][1])
    t = [[a * e[0][2] + b * e[1][2], a * e[0][3] + b * e[1][3]], [b * e[0][2] + c * e[1][2], b * e[0][3] + c * e[1][3]]]
    s22 = e[2][2] - (e[0][2] * t[0][0] + e[1][2] * t[1][0])
    s23 = e[2][3] - (e[0][2] * t[0][1] + e[1][2] * t[1][1])
    s33 = e[3][3] - (e[0][3] * t[0][1] + e[1][3] * t[1][1])
    f, g, h = pair_inverse(s22, s23, s33)
    w = [[t[0][0] * f + t[0][1] * g, t[0][0] * g + t[0][1] * h], [t[1][0] * f + t[1][1] * g, t[1][0] * g + t[1][1] * h]]
    i00 = a + w[0][0] * t[0][0] + w[0][1] * t[0][1]
    i01 = b + w[0][0] * t[1][0] + w[0][1] * t[1][1]
    i11 = c + w[1][0] * t[1][0] + w[1][1] * t[1][1]
    return [
        [i00, i01, -w[0][0], -w[0][1]],
        [i01, i11, -w[1][0], -w[1][1]],
        [-w[0][0], -w[1][0], f, g],
        [-w[0][1], -w[1][1], g, h],
    ]


def spd_inverse(normal, block=16):
    pivots = 4
    count = normal.shape[0]
    lane = lax.broadcasted_iota(jnp.int32, (1, count), 1)
    sub = lax.broadcasted_iota(jnp.int32, (block, 1), 0)
    for first in range(0, count, block):
        panel = normal[first:first + block, :]
        for i in range(0, block, pivots):
            k = first + i
            cols = [jnp.broadcast_to(panel[:, k + m:k + m + 1], (block, count)) for m in range(pivots)]
            entry = [[jnp.broadcast_to(cols[n][i + m:i + m + 1, :], (8, count)) for n in range(pivots)] for m in range(pivots)]
            q = quad_inverse(entry)
            inside = jnp.logical_and(lane >= k, lane < k + pivots)
            rows = [
                jnp.where(inside, jnp.where(lane == k + m, 1.0, 0.0), jnp.broadcast_to(panel[i + m:i + m + 1, :], (8, count)))
                for m in range(pivots)
            ]
            new = [q[m][0] * rows[0] + (q[m][1] * rows[1] + (q[m][2] * rows[2] + q[m][3] * rows[3])) for m in range(pivots)]
            new = [jnp.concatenate([row] * (block // 8), axis=0) for row in new]
            panel = jnp.where(inside, 0.0, panel)
            for m in range(pivots):
                panel = panel - cols[m] * new[m]
            for m in range(pivots):
                panel = jnp.where(sub == i + m, new[m], panel)
        within = jnp.logical_and(lane >= first, lane < first + block)
        outer = jnp.dot(normal[:, first:first + block], panel, precision=HIGHEST, preferred_element_type=jnp.float32)
        rest = jnp.where(within, 0.0, normal) - outer
        above = [rest[:first]] if first > 0 else []
        below = [rest[first + block:]] if first + block < count else []
        normal = jnp.concatenate(above + [panel] + below, axis=0)
    return normal


def solve_kernel(narrow, *refs):
    left_ref, buffer_ref, sem = refs[-3:]
    touched_refs, response_refs = refs[:-3 - narrow], refs[-3 - narrow:-3]
    copies = []
    for i, ref in enumerate(response_refs):
        copies.append(pltpu.make_async_copy(ref, buffer_ref.at[i], sem.at[i]))
        copies[i].start()
    touched = touched_refs[0][...]
    for ref in touched_refs[1:]:
        touched = touched + ref[...]
    count = touched.shape[0]
    row = lax.broadcasted_iota(jnp.int32, (count, count), 0)
    column = lax.broadcasted_iota(jnp.int32, (count, count), 1)
    capacitance = jnp.where(row == column, 1.0, 0.0) - touched
    normal = lax.dot_general(
        capacitance, capacitance, (((1,), (1,)), ((), ())), precision=HIGHEST, preferred_element_type=jnp.float32
    )
    inverse = jnp.dot(spd_inverse(normal), capacitance, precision=HIGHEST, preferred_element_type=jnp.float32)
    for copy in copies:
        copy.wait()
    response = buffer_ref[0]
    for i in range(1, narrow):
        response = response + buffer_ref[i]
    solved = lax.dot_general(
        response, inverse, (((1,), (1,)), ((), ())), precision=HIGHEST, preferred_element_type=jnp.float32
    )
    s_high, s_low = split(solved)
    left_ref[...] = jnp.concatenate([s_high, s_low, s_high], axis=1)


def solve(touched, response):
    rows, count = response[0].shape
    narrow = len(response)
    vmem = pl.BlockSpec(memory_space=pltpu.VMEM)
    return pl.pallas_call(
        functools.partial(solve_kernel, narrow),
        out_shape=jax.ShapeDtypeStruct((rows, 3 * count), jnp.bfloat16),
        in_specs=[vmem] * len(touched) + [pl.BlockSpec(memory_space=pl.ANY)] * narrow,
        out_specs=vmem,
        scratch_shapes=[pltpu.VMEM((narrow, rows, count), jnp.float32), pltpu.SemaphoreType.DMA((narrow,))],
        cost_estimate=pl.CostEstimate(flops=2_000_000_000, bytes_accessed=8_000_000, transcendentals=0),
        compiler_params=pltpu.CompilerParams(vmem_limit_bytes=16 * 1024 * 1024),
        name="solve",
    )(*touched, *response)


def places(core, part):
    x = (lax.axis_index("wide") // CORES) % XS
    return [pl.ds(pl.multiple_of((lax.rem(x + (XS - d), XS) * CORES + core) * part, part), part) for d in range(XS)]


def write_blocks(left, g_ref, pieces, out_ref, buffer_ref, sem, core):
    copies = []
    for d, here in enumerate(places(core, pieces[0].shape[1])):
        r_high, r_low = split(pieces[d][...])
        right = jnp.concatenate([r_high, r_high, r_low], axis=0)
        buffer_ref[d] = g_ref[:, here] + jnp.dot(left, right, preferred_element_type=jnp.float32)
        copies.append(pltpu.make_async_copy(buffer_ref.at[d], out_ref.at[:, here], sem.at[d]))
        copies[d].start()
    for copy in copies:
        copy.wait()


def update_own_kernel(left_ref, g_ref, *refs):
    pieces, (out_ref, buffer_ref, sem) = refs[:XS], refs[XS:]
    write_blocks(left_ref[...], g_ref, pieces, out_ref, buffer_ref, sem, lax.axis_index("wide") % CORES)


def update_other_kernel(left_ref, g_ref, before_ref, *refs):
    pieces, (out_ref, buffer_ref, sem) = refs[:XS], refs[XS:]
    write_blocks(left_ref[...], g_ref, pieces, out_ref, buffer_ref, sem, 1 - lax.axis_index("wide") % CORES)


def update(gebhart, left, pieces, swapped):
    rows, nodes = gebhart.shape
    part = pieces[0].shape[1]
    vmem = pl.BlockSpec(memory_space=pltpu.VMEM)
    hbm = pl.BlockSpec(memory_space=pl.ANY)
    whole = jax.ShapeDtypeStruct((rows, nodes), jnp.float32)
    scratch = [pltpu.VMEM((XS, rows, part), jnp.float32), pltpu.SemaphoreType.DMA((XS,))]
    params = pltpu.CompilerParams(vmem_limit_bytes=16 * 1024 * 1024)
    own = pl.pallas_call(
        update_own_kernel,
        out_shape=whole,
        in_specs=[vmem] * (2 + XS),
        out_specs=hbm,
        scratch_shapes=scratch,
        cost_estimate=pl.CostEstimate(flops=1_000_000_000, bytes_accessed=6_000_000, transcendentals=0),
        compiler_params=params,
        name="update_own",
    )(left, gebhart, *pieces)
    return pl.pallas_call(
        update_other_kernel,
        out_shape=whole,
        in_specs=[vmem, vmem, hbm] + [vmem] * XS,
        out_specs=hbm,
        scratch_shapes=scratch,
        input_output_aliases={2: 0},
        compiler_params=params,
        name="update_other",
    )(left, gebhart, own, *swapped)


def body(wide, narrow, gebhart, change, moved_nodes):
    rows_local, width_local = gebhart.shape
    count = moved_nodes.shape[0]
    half = count // CORES
    zs = wide // (CORES * XS)
    width = width_local // XS
    group = half // zs
    me = lax.axis_index("wide")
    core = me % CORES
    x = (me // CORES) % XS
    z = me // (CORES * XS)

    def index(z, x, c):
        return (z * XS + x) * CORES + c

    places = [(z, x, c) for z in range(zs) for x in range(XS) for c in range(CORES)]
    swap = [(index(z, x, c), index(z, x, (c + 1) % CORES)) for z, x, c in places]
    shift_x = [[(index(z, x, c), index(z, (x + d) % XS, c)) for z, x, c in places] for d in range(XS)]
    shift_y = [[(i, (i + d) % narrow) for i in range(narrow)] for d in range(narrow)]
    x_groups = [[index(z, x, c) for x in range(XS)] for z in range(zs) for c in range(CORES)]
    z_groups = [[index(z, x, c) for z in range(zs)] for x in range(XS) for c in range(CORES)]

    part = width // CORES
    picked, table = pick_slots(gebhart, change, moved_nodes)

    def received(value):
        return [lax.ppermute(value, "narrow", shift_y[d]) for d in range(1, narrow)]

    own = [picked[0]] + [lax.ppermute(picked[d], "wide", shift_x[d]) for d in range(1, XS)]
    other = [lax.ppermute(slots, "wide", swap) for slots in own]

    def spread(room, gebhart, change, moved_nodes, slots, table):
        slots = plane_slots(table, slots, zs, room)
        slots, token = lax.optimization_barrier((slots, table))
        partial_value = respond(token, gebhart, change)
        response = [partial_value] + received(partial_value)
        slots = lax.all_to_all(slots, "wide", 0, 0, axis_index_groups=z_groups)
        slots, response = lax.optimization_barrier((slots, response))
        return tuple(order(table, slots.reshape(zs * room, part + count))) + tuple(response)

    def crowded(gebhart, change, moved_nodes, slots, table):
        partial_value = respond(table, gebhart, change)
        owner = moved_nodes // rows_local
        owner_half = lax.dynamic_slice(owner, (core * half,), (half,))
        owner_core = owner_half % CORES
        owner_x = (owner_half // CORES) % XS
        owner_z = lax.dynamic_slice(owner_half // (CORES * XS), (z * group,), (group,))

        keep, send = pick_all(gebhart, moved_nodes, half, width)
        got = lax.ppermute(send, "wide", swap)
        positions = me * rows_local + lax.broadcasted_iota(jnp.int32, (count, rows_local), 1)
        select = (moved_nodes[:, None] == positions).astype(jnp.float32)
        terms = jnp.dot(select, partial_value, preferred_element_type=jnp.float32, precision=HIGHEST)
        terms_mine = lax.dynamic_slice(terms, (core * half, 0), (half, count))
        terms_theirs = lax.dynamic_slice(terms, ((1 - core) * half, 0), (half, count))
        terms_chip = terms_mine + lax.ppermute(terms_theirs, "wide", swap)

        rows_chip = jnp.where((owner_core == core)[None, :, None], keep, got)
        both = jnp.concatenate([rows_chip, jnp.broadcast_to(terms_chip[None], (XS, half, count))], axis=2)
        both = lax.all_to_all(both, "wide", 0, 0, axis_index_groups=x_groups)
        chosen = owner_x[None, :, None] == lax.broadcasted_iota(jnp.int32, (XS, 1, 1), 0)
        both = jnp.sum(jnp.where(chosen, both, 0.0), axis=0)

        both = lax.all_to_all(both.reshape(zs, group, width + count), "wide", 0, 0, axis_index_groups=z_groups)
        chosen = owner_z[None, :, None] == lax.broadcasted_iota(jnp.int32, (zs, 1, 1), 0)
        both = jnp.sum(jnp.where(chosen, both, 0.0), axis=0)
        both = lax.all_to_all(jnp.broadcast_to(both[None], (zs,) + both.shape), "wide", 0, 0, axis_index_groups=z_groups)
        both = both.reshape(half, width + count)

        mine = jnp.concatenate([lax.dynamic_slice(both, (0, core * part), (half, part)), both[:, width:]], axis=1)
        theirs = jnp.concatenate([lax.dynamic_slice(both, (0, (1 - core) * part), (half, part)), both[:, width:]], axis=1)
        theirs = lax.ppermute(theirs, "wide", swap)
        both = jnp.where(core == 0, jnp.concatenate([mine, theirs]), jnp.concatenate([theirs, mine]))
        return (both[:, :part], both[:, part:], partial_value) + tuple(received(partial_value))

    paths = [functools.partial(spread, room) for room in PLANES] + [crowded]
    rows, touched, *response = lax.switch(table[2, 0], paths, gebhart, change, moved_nodes, own + other, table)

    pieces = [rows] + [lax.ppermute(rows, "wide", shift_x[d]) for d in range(1, XS)]
    step = 1
    while step < narrow:
        parts = [touched, lax.ppermute(touched, "narrow", [(i, i ^ (2 * step - 1)) for i in range(narrow)])]
        touched = parts[0] + parts[1]
        step *= 2
    left = solve(parts, response)
    pieces, left = lax.optimization_barrier((pieces, left))
    return update(gebhart, left, pieces, [lax.ppermute(piece, "wide", swap) for piece in pieces])


def solution(mesh):
    return jax.shard_map(
        functools.partial(body, mesh.shape["wide"], mesh.shape["narrow"]),
        mesh=mesh,
        in_specs=(P("wide", "narrow"), P("narrow", None), P()),
        out_specs=P("wide", "narrow"),
        check_vma=False,
    )
```
